256 devices in a mesh: dp: 32 (over z, y), mem: 8 (over x, core).
Axes of the slice: x: 4, y: 4, z: 8, core: 2. Of those that a mesh axis runs over, the one named last changes fastest.
Arguments:
- modelled_reactions: bfloat16 [98304, 2048], P('dp', 'mem'), may hold values from -6 to 6
- observations: float32 [98304], P('dp'), may hold values from -6 to 6
- noise_class: int32 [98304], P('dp'), may hold values from 0 to 7
- class_variance: float32 [8], replicated, may hold values from 0.25 to 4
- ensemble: float32 [64, 2048], P(None, 'mem'), may hold values from -18 to 18
Outputs:
- updated: float32 [64, 2048], P(None, 'mem')
The draws below stay inside these ranges and needn't reach their ends.
All inputs are finite; a program needn't handle non-finite values.
Results may differ from the reference program's by a relative error of at most 0.0003.
The reference program's roundings to bfloat16 on the way count: a program that leaves them out, or rounds other values in their place, can miss the bound.
Values may be sent and summed in bfloat16 or wider, within the bound.
A program may use at most 64 MiB of HBM per device.

```python
import math
import jax
import jax.numpy as jnp
from jax import lax

ENSEMBLE_SIZE = 2048
P_SIZE = 64
K = 8
ITERS = 2
ROWS_DEV = 3072
N = 98304
N_DP = 32


def draw_modelled_reactions(key, part):
    key = jax.random.fold_in(key, 11)
    entry_key = jax.random.fold_in(key, 1)
    values = jax.random.truncated_normal(entry_key, -6.0, 6.0, (N, ENSEMBLE_SIZE), jnp.float32)
    return values.astype(jnp.bfloat16)


def set_ends(drawn, own_key, least, high):
    place = [jax.random.randint(jax.random.fold_in(own_key, axis), (), 0, length) for axis, length in enumerate(drawn.shape)]
    main_axis = drawn.shape.index(max(drawn.shape))
    next_to = place[:main_axis] + [(place[main_axis] + 1) % drawn.shape[main_axis]] + place[main_axis + 1:]
    return drawn.at[tuple(place)].set(least).at[tuple(next_to)].set(high)


def shard_levels(own_key, extent, shards, smallest, high):
    loudness = 1.0
    for axis_at, blocks in shards:
        steps = jax.random.uniform(jax.random.fold_in(jax.random.fold_in(own_key, 6), axis_at), (blocks,), jnp.float32, smallest / len(shards), high / len(shards))
        loudness = loudness * jnp.repeat(jnp.exp(steps), extent[axis_at] // blocks).reshape((-1,) + (1,) * (len(extent) - 1 - axis_at))
    return loudness


def gaussian(rng, extent, deviation, most, cuts=(), kind=jnp.bfloat16):
    array = deviation * jax.random.normal(rng, extent, jnp.float32)
    if cuts:
        array = array * shard_levels(rng, extent, cuts, -0.22, 0.18)
    return jnp.clip(array, -most, most).astype(kind)


def setup_inputs(seed: int = 0) -> dict:
    key_of = jax.random.split(jax.random.key(seed), 6)
    return {
        "modelled_reactions": draw_modelled_reactions(jax.random.fold_in(key_of[5], 71), 0),
        "observations": gaussian(key_of[1], (N,), 1.0, 6.0, ((0, 32),), jnp.float32),
        "noise_class": set_ends(jax.random.randint(key_of[2], (N,), 0, K), jax.random.fold_in(key_of[2], 1), 0, K - 1).astype(jnp.int32),
        "class_variance": jnp.clip(jnp.exp(jax.random.uniform(key_of[3], (K,), jnp.float32, math.log(0.25), math.log(4.0))), 0.25, 4.0),
        "ensemble": gaussian(key_of[4], (P_SIZE, ENSEMBLE_SIZE), 3.0, 18.0, ((1, 8),), jnp.float32),
    }


def reference(modelled_reactions, observations, noise_class, class_variance, ensemble):
    levels = jnp.arange(K, dtype=jnp.int32)
    variance = lax.optimization_barrier(jnp.sum(jnp.where(noise_class[:, None] == levels[None, :], class_variance[None, :], 0.0), axis=1))
    weight = lax.rsqrt(variance)
    blocks = (modelled_reactions.reshape(N_DP, ROWS_DEV, ENSEMBLE_SIZE), observations.reshape(N_DP, ROWS_DEV), weight.reshape(N_DP, ROWS_DEV))

    def accumulate(carry, item):
        particle_group, measured, factor = item
        prior_parameter_vector = particle_group.astype(jnp.float32)
        sample_average = lax.optimization_barrier(jnp.sum(prior_parameter_vector, axis=1)) / ENSEMBLE_SIZE
        normalised_deviation = factor / math.sqrt(ENSEMBLE_SIZE - 1)
        decorrelated_lines = ((prior_parameter_vector - sample_average[:, None]) * normalised_deviation[:, None]).astype(jnp.bfloat16)
        innovation = factor * (measured - sample_average)
        gram = carry[0] + lax.dot_general(decorrelated_lines, decorrelated_lines, (((0,), (0,)), ((), ())), preferred_element_type=jnp.float32)
        projected = carry[1] + jnp.dot(innovation, decorrelated_lines.astype(jnp.float32), precision=lax.Precision.HIGHEST)
        return ((gram, projected), None)
    start = (jnp.zeros((ENSEMBLE_SIZE, ENSEMBLE_SIZE), jnp.float32), jnp.zeros((ENSEMBLE_SIZE,), jnp.float32))
    (gram, projected), _ = lax.scan(accumulate, start, blocks)
    norm_scale = (ENSEMBLE_SIZE + jnp.trace(gram)) / ENSEMBLE_SIZE
    identity = jnp.eye(ENSEMBLE_SIZE, dtype=jnp.float32)
    current = (gram + identity) / norm_scale
    inverse = identity
    for sweep in range(ITERS):
        product = jnp.dot(inverse, current, precision=lax.Precision.HIGHEST)
        update = 1.5 * identity - 0.5 * product
        current = jnp.dot(current, update, precision=lax.Precision.HIGHEST)
        inverse = jnp.dot(inverse, update, precision=lax.Precision.HIGHEST)
    center = lax.optimization_barrier(jnp.sum(ensemble, axis=1)) / ENSEMBLE_SIZE
    anomaly = ensemble - center[:, None]
    weighted = jnp.dot(inverse, projected, precision=lax.Precision.HIGHEST)
    shares = jnp.dot(weighted, inverse, precision=lax.Precision.HIGHEST) / norm_scale
    shift = jnp.dot(anomaly, shares, precision=lax.Precision.HIGHEST) / math.sqrt(ENSEMBLE_SIZE - 1)
    moved = jnp.dot(anomaly, inverse, precision=lax.Precision.HIGHEST)
    return center[:, None] + shift[:, None] + moved / jnp.sqrt(norm_scale)
```

```python
import functools
import math

import jax
import jax.numpy as jnp
from jax import lax
from jax.experimental import pallas as pl
from jax.experimental.pallas import tpu as pltpu
from jax.sharding import PartitionSpec as P

MESH = pl.DeviceIdType.MESH
HIGHEST = lax.Precision.HIGHEST
NX, NY, NZ, NM = 4, 4, 8, 8
MEMBERS = 2048
CM = 256
NS = 3072
HALF = NS // 2
KT = 512
CHUNKS = (64, 64, 64, 32, 32)
STARTS = tuple(sum(CHUNKS[:i]) for i in range(len(CHUNKS)))
ROWS = (CM,) + tuple(2 * part for part in CHUNKS)
N_SEMS = 7 + 7 + 1 + 3 * len(CHUNKS) + 17 + 20 * len(ROWS) + 28 + 10
NT = (((1,), (1,)), ((), ()))


def piece(rows, index):
    groups = rows // 4 // 8
    lanes = NZ // groups
    width = 512 // lanes
    return (
        pl.ds(pl.multiple_of((index // lanes) * 8, 8), 8),
        pl.ds(pl.multiple_of((index % lanes) * width, 128), width),
    )


def piece_shape(rows):
    return (8, 512 // (NZ // (rows // 4 // 8)))


def kernel(var_ref, m_ref, obs_ref, cls_ref, ens_ref, out_ref, *scratch):
    (
        raw, relay, near, far, sib, white, sums, scale, bases, ensemble_in, centers,
        small, small_y, small_z, small_m, strip, vec, polys, exchange, rows_out, sems,
    ) = scratch[:21]
    lists = scratch[21:]
    n = len(ROWS)
    part, from_y, sum_y, from_z, gather_z = (lists[i * n : (i + 1) * n] for i in range(5))

    dp, mem = lax.axis_index("dp"), lax.axis_index("mem")
    z, y = dp // NY, dp % NY
    c, k = mem // 2, mem % 2

    def mem_at(offset):
        return (dp, (mem + offset) % NM)

    def x_at(offset):
        return (dp, ((c + offset + NX) % NX) * 2 + k)

    def y_at(offset):
        return (z * NY + (y + offset) % NY, mem)

    def z_at(offset):
        return (((z + offset) % NZ) * NY + y, mem)

    used = [0]
    pending = []

    def remote(src, dst, device):
        i = used[0]
        used[0] += 1
        return pltpu.make_async_remote_copy(
            src_ref=src,
            dst_ref=dst,
            send_sem=sems.at[0, i],
            recv_sem=sems.at[1, i],
            device_id=device,
            device_id_type=MESH,
        )

    def start(copies):
        for copy in copies:
            copy.start()
            pending.append(copy)

    def arrive(copies):
        for copy in copies:
            copy.wait_recv()

    def drain():
        while pending:
            pending.pop(0).wait_send()

    barrier = pltpu.get_barrier_semaphore()
    greeted = (
        [mem_at(j) for j in range(1, NM)]
        + [y_at(j) for j in range(1, NY)]
        + [z_at(j) for j in range(1, NZ)]
    )
    for device in greeted:
        pl.semaphore_signal(barrier, inc=1, device_id=device, device_id_type=MESH)

    eye = (
        lax.broadcasted_iota(jnp.int32, (CM, CM), 0) == lax.broadcasted_iota(jnp.int32, (CM, CM), 1)
    )
    turn = jnp.concatenate(
        [jnp.where(eye, 1.0, 0.0), jnp.ones((16, CM), jnp.float32)], axis=0
    ).astype(jnp.bfloat16)

    @pl.loop(0, NS // KT)
    def _(i):
        at = pl.ds(pl.multiple_of(i * KT, KT), KT)
        turned = lax.dot_general(turn, m_ref[at, :], NT, preferred_element_type=jnp.float32)
        raw[:, at] = turned[:CM].astype(jnp.bfloat16)
        bases[:, at] = turned[CM : CM + 1]

    sums[mem] = bases[...]
    group = pl.ds(pl.multiple_of(z * 8, 8), 8)
    ensemble_in[mem] = ens_ref[group, :]

    pl.semaphore_wait(barrier, len(greeted))

    sum_copies = [remote(sums.at[mem], sums.at[mem], mem_at(j)) for j in range(1, NM)]
    start(sum_copies)
    sib_copy = remote(raw, sib, (dp, mem + 1 - 2 * k))
    start([sib_copy])
    near_copies, relay_copies, far_copies = [], [], []
    half_of_far = pl.multiple_of((1 - c // 2) * HALF, HALF)
    for first, count in zip(STARTS, CHUNKS, strict=True):
        at = pl.ds(first, count)
        near_copies.append(remote(raw.at[at], near.at[at], x_at(-1)))
        relay_copies.append(remote(raw.at[at, pl.ds(half_of_far, HALF)], relay.at[at], x_at(1)))
        far_copies.append(remote(relay.at[at], far.at[at], x_at(1)))
    for i in range(2):
        start([near_copies[i], relay_copies[i]])
    ens_copies = [
        remote(ens_ref.at[group], ensemble_in.at[mem], mem_at(j)) for j in range(1, NM)
    ]
    start(ens_copies)

    classes = cls_ref[...]
    variance = jnp.zeros((1, NS), jnp.float32)
    for level in range(8):
        variance = jnp.where(classes == level, var_ref[level], variance)
    weight = lax.rsqrt(variance)
    scale[...] = weight / math.sqrt(MEMBERS - 1)

    arrive(sum_copies)
    total = sums[0]
    for j in range(1, NM):
        total = total + sums[j]
    average = total / MEMBERS
    bases[...] = average
    innovation = weight * (obs_ref[...] - average)

    def whiten(block, at):
        return (
            (block.astype(jnp.float32) - bases[:, at]) * scale[:, at]
        ).astype(jnp.bfloat16)

    own = pl.ds(pl.multiple_of(k * CM, CM), CM)
    other = pl.ds(pl.multiple_of((1 - k) * CM, CM), CM)
    for i in range(NS // KT):
        at = pl.ds(i * KT, KT)
        white[own, at] = whiten(raw[:, at], at)
    arrive([sib_copy])
    part[0][...] = jnp.zeros((CM, 512), jnp.float32)

    @pl.loop(0, NS // KT)
    def _(i):
        at = pl.ds(pl.multiple_of(i * KT, KT), KT)
        white[other, at] = whiten(sib[:, at], at)
        part[0][...] += lax.dot_general(
            white[own, at], white[:, at], NT, preferred_element_type=jnp.float32
        )

    def reduce_y(q):
        quarter = ROWS[q] // 4
        copies = []
        for j in range(1, NY):
            target = (y + j) % NY
            rows = pl.ds(pl.multiple_of(target * quarter, 8), quarter)
            copies.append(remote(part[q].at[rows], from_y[q].at[j - 1], y_at(j)))
        start(copies)
        return copies

    def reduce_z(q, copies):
        quarter = ROWS[q] // 4
        arrive(copies)
        mine = pl.ds(pl.multiple_of(y * quarter, 8), quarter)
        sum_y[q][...] = part[q][mine, :] + from_y[q][0] + from_y[q][1] + from_y[q][2]
        copies = []
        for j in range(1, NZ):
            rows, lanes = piece(ROWS[q], (z + j) % NZ)
            copies.append(remote(sum_y[q].at[rows, lanes], from_z[q].at[j - 1], z_at(j)))
        start(copies)
        return copies

    def spread_z(q, copies):
        arrive(copies)
        rows, lanes = piece(ROWS[q], z)
        total = sum_y[q][rows, lanes]
        for j in range(NZ - 1):
            total = total + from_z[q][j]
        gather_z[q][rows, lanes] = total
        here = gather_z[q].at[rows, lanes]
        copies = [remote(here, here, z_at(j)) for j in range(1, NZ)]
        start(copies)
        return copies

    def spread_y(q, copies):
        quarter = ROWS[q] // 4
        arrive(copies)
        if q == 0:
            first = y * quarter
        else:
            first = CM + (y // 2) * CM + STARTS[q - 1] + (y % 2) * quarter
        rows = pl.ds(pl.multiple_of(first, 8), quarter)
        strip[rows, :] = gather_z[q][...]
        copies = [remote(gather_z[q], strip.at[rows], y_at(j)) for j in range(1, NY)]
        start(copies)
        return copies

    half = pl.multiple_of((c // 2) * HALF, HALF)

    def gram_part(q):
        i = q - 1
        first, count = STARTS[i], CHUNKS[i]
        at_rows = pl.ds(first, count)
        arrive([near_copies[i]])
        if i + 1 < len(CHUNKS):
            arrive([relay_copies[i + 1]])
            start([far_copies[i + 1]])
        if i + 2 < len(CHUNKS):
            start([near_copies[i + 2], relay_copies[i + 2]])
        part[q][...] = jnp.zeros((2 * count, 512), jnp.float32)

        @pl.loop(0, NS // KT)
        def _(s):
            at = pl.ds(pl.multiple_of(s * KT, KT), KT)
            part[q][:count] += lax.dot_general(
                whiten(near[at_rows, at], at), white[:, at], NT, preferred_element_type=jnp.float32
            )

        arrive([far_copies[i]])

        @pl.loop(0, HALF // KT)
        def _(s):
            here = pl.ds(pl.multiple_of(s * KT, KT), KT)
            at = pl.ds(pl.multiple_of(half + s * KT, KT), KT)
            part[q][count:] += lax.dot_general(
                whiten(far[at_rows, here], at), white[:, at], NT, preferred_element_type=jnp.float32
            )

    stages = [reduce_z, spread_z, spread_y, lambda q, copies: arrive(copies)]
    state = {0: reduce_y(0)}
    arrive([relay_copies[0]])
    start([far_copies[0]])

    high = innovation.astype(jnp.bfloat16)
    rest = innovation - high.astype(jnp.float32)
    middle = rest.astype(jnp.bfloat16)
    low = (rest - middle.astype(jnp.float32)).astype(jnp.bfloat16)
    split = jnp.concatenate(
        [
            high.astype(jnp.float32),
            middle.astype(jnp.float32),
            low.astype(jnp.float32),
            jnp.zeros((13, NS), jnp.float32),
        ],
        axis=0,
    ).astype(jnp.bfloat16)
    shadow = lax.dot_general(split, white[own, :], NT, preferred_element_type=jnp.float32)
    diagonal = jnp.sum(
        jnp.where(eye, part[0][:, pl.ds(pl.multiple_of(k * CM, CM), CM)], 0.0), axis=0, keepdims=True
    )
    small[...] = jnp.concatenate(
        [jnp.sum(shadow[:8], axis=0, keepdims=True), diagonal, jnp.zeros((6, CM), jnp.float32)], axis=0
    )
    small_copies = [remote(small, small_y.at[j - 1], y_at(j)) for j in range(1, NY)]
    start(small_copies)

    def small_sum_y():
        arrive(small_copies)
        small_z[NZ - 1] = small[...] + small_y[0] + small_y[1] + small_y[2]
        copies = [remote(small_z.at[NZ - 1], small_z.at[j - 1], z_at(j)) for j in range(1, NZ)]
        start(copies)
        return copies

    def small_sum_z(copies):
        arrive(copies)
        total = small_z[0]
        for j in range(1, NZ):
            total = total + small_z[j]
        small_m[mem] = total
        copies = [remote(small_m.at[mem], small_m.at[mem], mem_at(j)) for j in range(1, NM)]
        start(copies)
        return copies

    def first_vectors(copies):
        arrive(ens_copies)
        arrive(copies)
        center = ensemble_in[0].sum(axis=1, keepdims=True)
        for j in range(1, NM):
            center = center + ensemble_in[j].sum(axis=1, keepdims=True)
        center = center / MEMBERS
        place = lax.broadcasted_iota(jnp.int32, (8, 1), 0)

        def own_rows(block):
            return [
                jnp.sum(jnp.where(place == 2 * y + i, block, 0.0), axis=0, keepdims=True)
                for i in range(2)
            ]

        centers[:2, :] = jnp.concatenate(own_rows(jnp.broadcast_to(center, (8, 128))), axis=0)
        for j in range(NM):
            vec[j] = jnp.concatenate(
                own_rows(ensemble_in[j] - center)
                + [small_m[j, 0:1, :], jnp.zeros((5, CM), jnp.float32)],
                axis=0,
            )

    small_state = None
    for t in range(1, n + len(stages)):
        for depth in range(len(stages), 0, -1):
            q = t - depth
            if 0 <= q < n:
                state[q] = stages[depth - 1](q, state[q])
        if t < n:
            gram_part(t)
            state[t] = reduce_y(t)
        if t == 1:
            small_state = small_sum_y()
        elif t == 2:
            small_state = small_sum_z(small_state)
        elif t == 3:
            first_vectors(small_state)

    trace = small_m[0, 1:2, :]
    for j in range(1, NM):
        trace = trace + small_m[j, 1:2, :]
    norm = (MEMBERS + jnp.sum(trace, axis=1, keepdims=True)) / MEMBERS

    next_one = ((c + 1) % NX) * 2 + k
    next_two = ((c + 2) % NX) * 2 + k

    def times(step):
        lhs = jnp.concatenate([vec[mem], vec[next_one], vec[next_two]], axis=1)
        exchange[step, mem, :, :512] = jnp.dot(
            lhs, strip[...], precision=HIGHEST, preferred_element_type=jnp.float32
        )
        lhs = jnp.concatenate([vec[2 * c], vec[2 * c + 1]], axis=1)
        exchange[step, mem, :, 512:] = lax.dot_general(
            lhs, strip[CM:, :], NT, precision=HIGHEST, preferred_element_type=jnp.float32
        )
        here = exchange.at[step, mem]
        copies = [remote(here, here, mem_at(j)) for j in range(1, NM)]
        start(copies)
        arrive(copies)
        result = []
        for chip in range(NX):
            for core in range(2):
                cols = slice(core * CM, (core + 1) * CM)
                product = (
                    exchange[step, 2 * chip, :, cols]
                    + exchange[step, 2 * chip + 1, :, cols]
                    + exchange[step, 2 * ((chip - 1) % NX) + core, :, 512:768]
                    + exchange[step, 2 * ((chip - 2) % NX) + core, :, 768:]
                )
                result.append((product + vec[2 * chip + core]) / norm)
        return result

    moved = times(0)
    for j in range(NM):
        vec[j] = 1.5 * vec[j] - 0.5 * moved[j]
        polys[j] = vec[j]
    moved = times(1)
    for j in range(NM):
        vec[j] = 1.5 * vec[j] - 0.5 * moved[j]
    moved = times(2)
    for j in range(NM):
        vec[j] = moved[j]
    moved = times(3)
    shift = jnp.zeros((2, 1), jnp.float32)
    for j in range(NM):
        applied = 1.5 * polys[j] - 0.5 * (1.5 * vec[j] - 0.5 * moved[j])
        polys[j] = applied
        shift = shift + jnp.sum(applied[:2] * applied[2:3], axis=1, keepdims=True)
    shift = shift / norm / math.sqrt(MEMBERS - 1)
    center = centers[:2, :1]
    rows_out[y, :2, :] = center + shift + polys[mem][:2] / jnp.sqrt(norm)
    here = rows_out.at[y]
    copies = [remote(here, here, y_at(j)) for j in range(1, NY)]
    start(copies)
    arrive(copies)
    out_ref[group, :] = jnp.concatenate([rows_out[j, :2, :] for j in range(NY)], axis=0)
    here = out_ref.at[group]
    copies = [remote(here, here, z_at(j)) for j in range(1, NZ)]
    start(copies)
    arrive(copies)
    drain()


def shards(modelled_reactions, observations, noise_class, class_variance, ensemble):
    f32, bf16 = jnp.float32, jnp.bfloat16
    vmem = pl.BlockSpec(memory_space=pltpu.VMEM)
    scratch = [
        pltpu.VMEM((CM, NS), bf16),
        pltpu.VMEM((CM, HALF), bf16),
        pltpu.VMEM((CM, NS), bf16),
        pltpu.VMEM((CM, HALF), bf16),
        pltpu.VMEM((CM, NS), bf16),
        pltpu.VMEM((2 * CM, NS), bf16),
        pltpu.VMEM((NM, 1, NS), f32),
        pltpu.VMEM((1, NS), f32),
        pltpu.VMEM((1, NS), f32),
        pltpu.VMEM((NM, 8, CM), f32),
        pltpu.VMEM((8, 128), f32),
        pltpu.VMEM((8, CM), f32),
        pltpu.VMEM((NY - 1, 8, CM), f32),
        pltpu.VMEM((NZ, 8, CM), f32),
        pltpu.VMEM((NM, 8, CM), f32),
        pltpu.VMEM((3 * CM, 512), f32),
        pltpu.VMEM((NM, 8, CM), f32),
        pltpu.VMEM((NM, 8, CM), f32),
        pltpu.VMEM((4, NM, 8, 1024), f32),
        pltpu.VMEM((NY, 8, CM), f32),
        pltpu.SemaphoreType.DMA((2, N_SEMS)),
    ]
    scratch += [pltpu.VMEM((r, 512), f32) for r in ROWS]
    scratch += [pltpu.VMEM((NY - 1, r // 4, 512), f32) for r in ROWS]
    scratch += [pltpu.VMEM((r // 4, 512), f32) for r in ROWS]
    scratch += [pltpu.VMEM((NZ - 1,) + piece_shape(r), f32) for r in ROWS]
    scratch += [pltpu.VMEM((r // 4, 512), f32) for r in ROWS]
    return pl.pallas_call(
        kernel,
        out_shape=jax.ShapeDtypeStruct((64, CM), f32),
        in_specs=[pl.BlockSpec(memory_space=pltpu.SMEM), vmem, vmem, vmem, vmem],
        out_specs=vmem,
        scratch_shapes=scratch,
        compiler_params=pltpu.CompilerParams(
            collective_id=0, has_side_effects=True, vmem_limit_bytes=40 * 1024 * 1024
        ),
    )(
        class_variance,
        modelled_reactions,
        observations.reshape(1, NS),
        noise_class.reshape(1, NS),
        ensemble,
    )


def solution(mesh):
    placed = (P("dp", "mem"), P("dp"), P("dp"), P(), P(None, "mem"))
    return jax.shard_map(
        shards, mesh=mesh, in_specs=placed, out_specs=P(None, "mem"), check_vma=False
    )
```

```python
import math

import jax
import jax.numpy as jnp
from jax import lax
from jax.experimental import pallas as pl
from jax.experimental.pallas import tpu as pltpu
from jax.sharding import PartitionSpec as P

MESH = pl.DeviceIdType.MESH
NX, NY, NZ, NM = 4, 4, 8, 8
MEMBERS = 2048
CM = 256
NS = 3072
HALF = NS // 2
KT = 512
CHUNKS = (128, 64, 32, 32)
STARTS = tuple(sum(CHUNKS[:i]) for i in range(len(CHUNKS)))
ROWS = (CM,) + tuple(2 * part for part in CHUNKS)
PREV = 2
VR = 4
WIDE = 5 * CM
N_SEMS = 7 + 7 + 1 + len(CHUNKS) + 2 * PREV + 17 + 20 * len(ROWS) + 28 + 10
N_LOADS = NS // KT + 4
NT = (((1,), (1,)), ((), ()))


def piece(rows, index):
    groups = rows // 4 // 8
    lanes = NZ // groups
    width = 512 // lanes
    return (
        pl.ds(pl.multiple_of((index // lanes) * 8, 8), 8),
        pl.ds(pl.multiple_of((index % lanes) * width, 128), width),
    )


def piece_shape(rows):
    return (8, 512 // (NZ // (rows // 4 // 8)))


def split_in_three(value):
    high = value.astype(jnp.bfloat16)
    rest = value - high.astype(jnp.float32)
    middle = rest.astype(jnp.bfloat16)
    return high, middle, (rest - middle.astype(jnp.float32)).astype(jnp.bfloat16)


def stacked(value, rows):
    terms = [term.astype(jnp.float32) for term in split_in_three(value)]
    spare = rows - 3 * value.shape[0]
    return jnp.concatenate(
        terms + [jnp.zeros((spare, value.shape[1]), jnp.float32)], axis=0
    ).astype(jnp.bfloat16)


def kernel(var_hbm, m_hbm, obs_hbm, cls_hbm, ens_hbm, out_ref, *scratch):
    (
        m_ref, obs_ref, cls_ref, var_ref, raw, near, prev, sib, white, white_prev, sums, scale, bases,
        ensemble_in, centers, small, small_y, small_z, small_m, strip, terms, vec, polys, exchange,
        rows_out, loads, sems,
    ) = scratch[:27]
    lists = scratch[27:]
    n = len(ROWS)
    part, from_y, sum_y, from_z, gather_z = (lists[i * n : (i + 1) * n] for i in range(5))

    dp, mem = lax.axis_index("dp"), lax.axis_index("mem")
    z, y = dp // NY, dp % NY
    c, k = mem // 2, mem % 2

    def mem_at(offset):
        return (dp, (mem + offset) % NM)

    def x_at(offset):
        return (dp, ((c + offset + NX) % NX) * 2 + k)

    def y_at(offset):
        return (z * NY + (y + offset) % NY, mem)

    def z_at(offset):
        return (((z + offset) % NZ) * NY + y, mem)

    sibling = (dp, mem + 1 - 2 * k)
    used = [0]
    pending = []

    def remote(src, dst, device):
        i = used[0]
        used[0] += 1
        return pltpu.make_async_remote_copy(
            src_ref=src,
            dst_ref=dst,
            send_sem=sems.at[0, i],
            recv_sem=sems.at[1, i],
            device_id=device,
            device_id_type=MESH,
        )

    def start(copies):
        for copy in copies:
            copy.start()
            pending.append(copy)

    def arrive(copies):
        for copy in copies:
            copy.wait_recv()

    def drain():
        while pending:
            pending.pop(0).wait_send()

    group = pl.ds(pl.multiple_of(z * 8, 8), 8)
    fetches = []
    for i in range(NS // KT):
        at = pl.ds(i * KT, KT)
        fetches.append(pltpu.make_async_copy(m_hbm.at[at], m_ref.at[at], loads.at[i]))
    for src, dst in (
        (cls_hbm, cls_ref),
        (obs_hbm, obs_ref),
        (var_hbm, var_ref),
        (ens_hbm.at[group], ensemble_in.at[mem]),
    ):
        fetches.append(pltpu.make_async_copy(src, dst, loads.at[len(fetches)]))
    for fetch in fetches:
        fetch.start()

    barrier = pltpu.get_barrier_semaphore()
    greeted = (
        [mem_at(j) for j in range(1, NM)]
        + [y_at(j) for j in range(1, NY)]
        + [z_at(j) for j in range(1, NZ)]
    )
    for device in greeted:
        pl.semaphore_signal(barrier, inc=1, device_id=device, device_id_type=MESH)

    eye = (
        lax.broadcasted_iota(jnp.int32, (CM, CM), 0) == lax.broadcasted_iota(jnp.int32, (CM, CM), 1)
    )
    turn = jnp.concatenate(
        [jnp.where(eye, 1.0, 0.0), jnp.ones((16, CM), jnp.float32)], axis=0
    ).astype(jnp.bfloat16)
    for i in range(NS // KT):
        at = pl.ds(i * KT, KT)
        fetches[i].wait()
        turned = lax.dot_general(turn, m_ref[at, :], NT, preferred_element_type=jnp.float32)
        raw[:, at] = turned[:CM].astype(jnp.bfloat16)
        sums[mem, :, at] = turned[CM : CM + 1]
    for fetch in fetches[NS // KT :]:
        fetch.wait()

    pl.semaphore_wait(barrier, len(greeted))

    own = pl.ds(pl.multiple_of(k * CM, CM), CM)
    other = pl.ds(pl.multiple_of((1 - k) * CM, CM), CM)
    sum_copies = [remote(sums.at[mem], sums.at[mem], mem_at(j)) for j in range(1, NM)]
    start(sum_copies)
    ens_copies = [
        remote(ensemble_in.at[mem], ensemble_in.at[mem], mem_at(j)) for j in range(1, NM)
    ]
    start(ens_copies)
    sib_copy = remote(raw, sib, sibling)
    start([sib_copy])
    near_copies = []
    for first, count in zip(STARTS, CHUNKS, strict=True):
        at = pl.ds(first, count)
        near_copies.append(remote(raw.at[at], near.at[at], x_at(-1)))
    next_half = pl.multiple_of((((c + 1) % NX) // 2) * HALF, HALF)
    prev_copies, shared_copies = [], []
    for i in range(PREV):
        rows = CM // PREV
        to_rows = pl.ds(pl.multiple_of(k * CM + i * rows, rows), rows)
        prev_copies.append(
            remote(
                raw.at[pl.ds(i * rows, rows), pl.ds(next_half, HALF)], prev.at[to_rows], x_at(1)
            )
        )
        shared_copies.append(remote(prev.at[to_rows], prev.at[to_rows], sibling))
    start(near_copies)
    start(prev_copies)

    classes = cls_ref[...]
    variance = jnp.zeros((1, NS), jnp.float32)
    for level in range(8):
        variance = jnp.where(classes == level, var_ref[level], variance)
    weight = lax.rsqrt(variance)
    scale[...] = weight / math.sqrt(MEMBERS - 1)

    arrive(sum_copies)
    total = sums[0]
    for j in range(1, NM):
        total = total + sums[j]
    average = total / MEMBERS
    bases[...] = average
    innovation = weight * (obs_ref[...] - average)

    def whiten(block, at):
        return ((block.astype(jnp.float32) - bases[:, at]) * scale[:, at]).astype(jnp.bfloat16)

    for i in range(NS // KT):
        at = pl.ds(i * KT, KT)
        white[own, at] = whiten(raw[:, at], at)
    arrive([sib_copy])
    part[0][...] = jnp.zeros((CM, 512), jnp.float32)

    @pl.loop(0, NS // KT)
    def _(i):
        at = pl.ds(pl.multiple_of(i * KT, KT), KT)
        white[other, at] = whiten(sib[:, at], at)
        part[0][...] += lax.dot_general(
            white[own, at], white[:, at], NT, preferred_element_type=jnp.float32
        )

    def reduce_y(q):
        quarter = ROWS[q] // 4
        copies = []
        for j in range(1, NY):
            target = (y + j) % NY
            rows = pl.ds(pl.multiple_of(target * quarter, 8), quarter)
            copies.append(remote(part[q].at[rows], from_y[q].at[j - 1], y_at(j)))
        start(copies)
        return copies

    def reduce_z(q, copies):
        quarter = ROWS[q] // 4
        arrive(copies)
        mine = pl.ds(pl.multiple_of(y * quarter, 8), quarter)
        sum_y[q][...] = part[q][mine, :] + from_y[q][0] + from_y[q][1] + from_y[q][2]
        copies = []
        for j in range(1, NZ):
            rows, lanes = piece(ROWS[q], (z + j) % NZ)
            copies.append(remote(sum_y[q].at[rows, lanes], from_z[q].at[j - 1], z_at(j)))
        start(copies)
        return copies

    def spread_z(q, copies):
        arrive(copies)
        rows, lanes = piece(ROWS[q], z)
        total = sum_y[q][rows, lanes]
        for j in range(NZ - 1):
            total = total + from_z[q][j]
        gather_z[q][rows, lanes] = total
        here = gather_z[q].at[rows, lanes]
        copies = [remote(here, here, z_at(j)) for j in range(1, NZ)]
        start(copies)
        return copies

    def spread_y(q, copies):
        quarter = ROWS[q] // 4
        arrive(copies)
        if q == 0:
            first = y * quarter
        else:
            first = CM + (y // 2) * CM + STARTS[q - 1] + (y % 2) * quarter
        rows = pl.ds(pl.multiple_of(first, 8), quarter)
        strip[rows, :] = gather_z[q][...]
        copies = [remote(gather_z[q], strip.at[rows], y_at(j)) for j in range(1, NY)]
        start(copies)
        return copies

    def finish(q, copies):
        arrive(copies)
        if q == 0:
            blocks = [(0, CM)]
        else:
            blocks = [(CM + STARTS[q - 1], CHUNKS[q - 1]), (2 * CM + STARTS[q - 1], CHUNKS[q - 1])]
        for first, count in blocks:
            at = pl.ds(first, count)
            for i, term in enumerate(split_in_three(strip[at, :])):
                terms[i, at, :] = term

    half = pl.multiple_of((c // 2) * HALF, HALF)

    def gram_part(q):
        i = q - 1
        first, count = STARTS[i], CHUNKS[i]
        at_rows = pl.ds(first, count)
        arrive([near_copies[i]])
        part[q][...] = jnp.zeros((2 * count, 512), jnp.float32)

        @pl.loop(0, NS // KT)
        def _(s):
            at = pl.ds(pl.multiple_of(s * KT, KT), KT)
            part[q][:count] += lax.dot_general(
                whiten(near[at_rows, at], at), white[:, at], NT, preferred_element_type=jnp.float32
            )

        @pl.loop(0, HALF // KT)
        def _(s):
            here = pl.ds(pl.multiple_of(s * KT, KT), KT)
            at = pl.ds(pl.multiple_of(half + s * KT, KT), KT)
            part[q][count:] += lax.dot_general(
                whiten(near[at_rows, at], at), white_prev[:, here], NT, preferred_element_type=jnp.float32
            )

        state[q] = reduce_y(q)

    state = {0: reduce_y(0)}

    shadow = lax.dot_general(
        stacked(innovation, 16), white[own, :], NT, preferred_element_type=jnp.float32
    )
    diagonal = jnp.sum(
        jnp.where(eye, part[0][:, pl.ds(pl.multiple_of(k * CM, CM), CM)], 0.0), axis=0, keepdims=True
    )
    small[...] = jnp.concatenate(
        [jnp.sum(shadow[:8], axis=0, keepdims=True), diagonal, jnp.zeros((6, CM), jnp.float32)], axis=0
    )
    small_copies = [remote(small, small_y.at[j - 1], y_at(j)) for j in range(1, NY)]
    start(small_copies)

    def small_sum_y(copies):
        arrive(copies)
        small_z[NZ - 1] = small[...] + small_y[0] + small_y[1] + small_y[2]
        copies = [remote(small_z.at[NZ - 1], small_z.at[j - 1], z_at(j)) for j in range(1, NZ)]
        start(copies)
        return copies

    def small_sum_z(copies):
        arrive(copies)
        total = small_z[0]
        for j in range(1, NZ):
            total = total + small_z[j]
        small_m[mem] = total
        copies = [remote(small_m.at[mem], small_m.at[mem], mem_at(j)) for j in range(1, NM)]
        start(copies)
        return copies

    def first_vectors(copies):
        arrive(ens_copies)
        arrive(copies)
        center = ensemble_in[0].sum(axis=1, keepdims=True)
        for j in range(1, NM):
            center = center + ensemble_in[j].sum(axis=1, keepdims=True)
        center = center / MEMBERS
        place = lax.broadcasted_iota(jnp.int32, (8, 1), 0)

        def own_rows(block):
            return [
                jnp.sum(jnp.where(place == 2 * y + i, block, 0.0), axis=0, keepdims=True)
                for i in range(2)
            ]

        centers[:2, :] = jnp.concatenate(own_rows(jnp.broadcast_to(center, (8, 128))), axis=0)
        for j in range(NM):
            vec[j] = jnp.concatenate(
                own_rows(ensemble_in[j] - center)
                + [small_m[j, 0:1, :], jnp.zeros((VR - 3, CM), jnp.float32)],
                axis=0,
            )

    def advance(stage, q):
        state[q] = stage(q, state[q])

    def share_prev(i):
        arrive([prev_copies[i]])
        start([shared_copies[i]])

    share_prev(0)
    small_state = small_sum_y(small_copies)
    advance(reduce_z, 0)
    small_state = small_sum_z(small_state)
    share_prev(1)
    arrive(shared_copies)

    @pl.loop(0, HALF // KT)
    def _(s):
        here = pl.ds(pl.multiple_of(s * KT, KT), KT)
        at = pl.ds(pl.multiple_of(half + s * KT, KT), KT)
        white_prev[:, here] = whiten(prev[:, here], at)

    gram_part(1)
    advance(spread_z, 0)
    gram_part(2)
    advance(reduce_z, 1)
    advance(spread_y, 0)
    gram_part(3)
    advance(spread_z, 1)
    advance(reduce_z, 2)
    gram_part(4)
    advance(reduce_z, 3)
    advance(spread_y, 1)
    advance(spread_z, 2)
    advance(finish, 0)
    advance(reduce_z, 4)
    advance(spread_z, 3)
    advance(spread_y, 2)
    advance(spread_z, 4)
    advance(spread_y, 3)
    first_vectors(small_state)
    advance(finish, 1)
    advance(spread_y, 4)
    advance(finish, 2)
    advance(finish, 3)
    advance(finish, 4)

    trace = small_m[0, 1:2, :]
    for j in range(1, NM):
        trace = trace + small_m[j, 1:2, :]
    norm = (MEMBERS + jnp.sum(trace, axis=1, keepdims=True)) / MEMBERS

    def folded(rows):
        return rows[:VR] + rows[VR : 2 * VR] + rows[2 * VR : 3 * VR]

    def times(step):
        ahead = vec[((c + 1) % NX) * 2 + k]
        behind = ((c + NX - 1) % NX) * 2
        down = stacked(jnp.concatenate([vec[mem], ahead], axis=1), 4 * VR)
        across = stacked(jnp.concatenate([vec[2 * c], vec[2 * c + 1]], axis=1), 4 * VR)
        back = stacked(jnp.concatenate([vec[behind], vec[behind + 1]], axis=1), 4 * VR)
        for_next = for_own = for_last = 0.0
        for i in range(3):
            for_next = (
                for_next
                + lax.dot_general(
                    across, terms[i, CM : 2 * CM, :], NT, preferred_element_type=jnp.float32
                )
                + lax.dot_general(
                    back, terms[i, 2 * CM :, :], NT, preferred_element_type=jnp.float32
                )
            )
            for_own = for_own + jnp.dot(
                down, terms[i, : 2 * CM, :], preferred_element_type=jnp.float32
            )
            for_last = for_last + jnp.dot(
                down[:, CM:], terms[i, 2 * CM :, :], preferred_element_type=jnp.float32
            )
        exchange[step, mem, :, :CM] = folded(for_next)
        exchange[step, mem, :, CM : 3 * CM] = folded(for_own)
        exchange[step, mem, :, 3 * CM :] = folded(for_last)
        here = exchange.at[step, mem]
        copies = [remote(here, here, mem_at(j)) for j in range(1, NM)]
        start(copies)
        arrive(copies)
        result = []
        for chip in range(NX):
            for core in range(2):
                mine = slice((core + 1) * CM, (core + 2) * CM)
                last = slice((core + 3) * CM, (core + 4) * CM)
                above = 2 * ((chip + 1) % NX)
                product = (
                    exchange[step, 2 * ((chip - 1) % NX) + core, :, :CM]
                    + exchange[step, 2 * chip, :, mine]
                    + exchange[step, 2 * chip + 1, :, mine]
                    + exchange[step, above, :, last]
                    + exchange[step, above + 1, :, last]
                )
                result.append((product + vec[2 * chip + core]) / norm)
        return result

    moved = times(0)
    for j in range(NM):
        vec[j] = 1.5 * vec[j] - 0.5 * moved[j]
        polys[j] = vec[j]
    moved = times(1)
    for j in range(NM):
        vec[j] = 1.5 * vec[j] - 0.5 * moved[j]
    moved = times(2)
    for j in range(NM):
        vec[j] = moved[j]
    moved = times(3)
    shift = jnp.zeros((2, 1), jnp.float32)
    for j in range(NM):
        applied = 1.5 * polys[j] - 0.5 * (1.5 * vec[j] - 0.5 * moved[j])
        polys[j] = applied
        shift = shift + jnp.sum(applied[:2] * applied[2:3], axis=1, keepdims=True)
    shift = shift / norm / math.sqrt(MEMBERS - 1)
    rows_out[y, :2, :] = centers[:2, :1] + shift + polys[mem][:2] / jnp.sqrt(norm)
    here = rows_out.at[y]
    copies = [remote(here, here, y_at(j)) for j in range(1, NY)]
    start(copies)
    arrive(copies)
    out_ref[group, :] = jnp.concatenate([rows_out[j, :2, :] for j in range(NY)], axis=0)
    here = out_ref.at[group]
    copies = [remote(here, here, z_at(j)) for j in range(1, NZ)]
    start(copies)
    arrive(copies)
    drain()


def shards(modelled_reactions, observations, noise_class, class_variance, ensemble):
    f32, bf16 = jnp.float32, jnp.bfloat16
    hbm = pl.BlockSpec(memory_space=pltpu.HBM)
    scratch = [
        pltpu.VMEM((NS, CM), bf16),
        pltpu.VMEM((1, NS), f32),
        pltpu.VMEM((1, NS), jnp.int32),
        pltpu.SMEM((8,), f32),
        pltpu.VMEM((CM, NS), bf16),
        pltpu.VMEM((CM, NS), bf16),
        pltpu.VMEM((2 * CM, HALF), bf16),
        pltpu.VMEM((CM, NS), bf16),
        pltpu.VMEM((2 * CM, NS), bf16),
        pltpu.VMEM((2 * CM, HALF), bf16),
        pltpu.VMEM((NM, 1, NS), f32),
        pltpu.VMEM((1, NS), f32),
        pltpu.VMEM((1, NS), f32),
        pltpu.VMEM((NM, 8, CM), f32),
        pltpu.VMEM((8, 128), f32),
        pltpu.VMEM((8, CM), f32),
        pltpu.VMEM((NY - 1, 8, CM), f32),
        pltpu.VMEM((NZ, 8, CM), f32),
        pltpu.VMEM((NM, 8, CM), f32),
        pltpu.VMEM((3 * CM, 512), f32),
        pltpu.VMEM((3, 3 * CM, 512), bf16),
        pltpu.VMEM((NM, VR, CM), f32),
        pltpu.VMEM((NM, VR, CM), f32),
        pltpu.VMEM((4, NM, VR, WIDE), f32),
        pltpu.VMEM((NY, 8, CM), f32),
        pltpu.SemaphoreType.DMA((N_LOADS,)),
        pltpu.SemaphoreType.DMA((2, N_SEMS)),
    ]
    scratch += [pltpu.VMEM((r, 512), f32) for r in ROWS]
    scratch += [pltpu.VMEM((NY - 1, r // 4, 512), f32) for r in ROWS]
    scratch += [pltpu.VMEM((r // 4, 512), f32) for r in ROWS]
    scratch += [pltpu.VMEM((NZ - 1,) + piece_shape(r), f32) for r in ROWS]
    scratch += [pltpu.VMEM((r // 4, 512), f32) for r in ROWS]
    return pl.pallas_call(
        kernel,
        out_shape=jax.ShapeDtypeStruct((64, CM), f32),
        in_specs=[hbm] * 5,
        out_specs=pl.BlockSpec(memory_space=pltpu.VMEM),
        scratch_shapes=scratch,
        compiler_params=pltpu.CompilerParams(
            collective_id=0, has_side_effects=True, vmem_limit_bytes=40 * 1024 * 1024
        ),
    )(
        class_variance,
        modelled_reactions,
        observations.reshape(1, NS),
        noise_class.reshape(1, NS),
        ensemble,
    )


def solution(mesh):
    placed = (P("dp", "mem"), P("dp"), P("dp"), P(), P(None, "mem"))
    return jax.shard_map(
        shards, mesh=mesh, in_specs=placed, out_specs=P(None, "mem"), check_vma=False
    )
```

```python
import math

import jax
import jax.numpy as jnp
from jax import lax
from jax.experimental import pallas as pl
from jax.experimental.pallas import tpu as pltpu
from jax.sharding import PartitionSpec as P

MESH = pl.DeviceIdType.MESH
NX, NY, NZ, NM = 4, 4, 8, 8
MEMBERS = 2048
CM = 256
NS = 3072
HALF = NS // 2
KT = 512
CHUNKS = (64, 64, 64, 32, 32)
STARTS = tuple(sum(CHUNKS[:i]) for i in range(len(CHUNKS)))
PARTS = (
    ((0,), 0, 128, 0),
    ((0,), 128, 128, 0),
    ((1,), 0, 64, 1),
    ((1,), 64, 64, 2),
    ((2,), 0, 128, 2),
    ((1, 2), 128, 64, 3),
    ((1, 2), 192, 32, 4),
    ((1, 2), 224, 32, 5),
)
ROWS = tuple(len(blocks) * count for blocks, _, count, _ in PARTS)
ORDER = (
    (0, 0), (1, 0), "small", (2, 0), "prev 0", (2, 1), (0, 1), (1, 1), "prev 1", (3, 0), "white prev", (4, 0),
    (2, 2), "small y", (3, 1), (1, 2), (5, 0), (0, 2), (4, 1), (3, 2), "small z", (1, 3), (6, 0), (5, 1), (7, 0),
    (0, 3), (4, 2), (6, 1), (2, 3), (3, 3), (7, 1), (5, 2), (4, 3), (6, 2), (7, 2), (5, 3), (1, 4), (6, 3),
    "vectors", (7, 3), (0, 4), (4, 4), (6, 4), (5, 4), (3, 4), (2, 4), (7, 4),
)
PREV = 2
VR = 4
WIDE = 5 * CM
N_SEMS = 7 + 7 + 1 + len(CHUNKS) + 2 * PREV + 17 + 20 * len(ROWS) + 28 + 10
N_LOADS = NS // KT + 4
FAR_Z = (4, 3, 5, 2, 6, 1, 7)
NT = (((1,), (1,)), ((), ()))


def piece(rows, index):
    groups = rows // 4 // 8
    lanes = NZ // groups
    width = 512 // lanes
    return (
        pl.ds(pl.multiple_of((index // lanes) * 8, 8), 8),
        pl.ds(pl.multiple_of((index % lanes) * width, 128), width),
    )


def piece_shape(rows):
    return (8, 512 // (NZ // (rows // 4 // 8)))


def split_in_three(value):
    high = value.astype(jnp.bfloat16)
    rest = value - high.astype(jnp.float32)
    middle = rest.astype(jnp.bfloat16)
    return high, middle, (rest - middle.astype(jnp.float32)).astype(jnp.bfloat16)


def stacked(value, rows):
    terms = [term.astype(jnp.float32) for term in split_in_three(value)]
    spare = rows - 3 * value.shape[0]
    return jnp.concatenate(
        terms + [jnp.zeros((spare, value.shape[1]), jnp.float32)], axis=0
    ).astype(jnp.bfloat16)


def kernel(var_hbm, m_hbm, obs_hbm, cls_hbm, ens_hbm, out_ref, *scratch):
    (
        m_ref, obs_ref, cls_ref, var_ref, raw, near, prev, sib, white, white_prev, sums, scale, bases,
        ensemble_in, centers, small, small_y, small_z, small_m, strip, terms, vec, polys, exchange,
        rows_out, loads, sems,
    ) = scratch[:27]
    lists = scratch[27:]
    n = len(ROWS)
    part, from_y, sum_y, from_z, gather_z = (lists[i * n : (i + 1) * n] for i in range(5))

    dp, mem = lax.axis_index("dp"), lax.axis_index("mem")
    z, y = dp // NY, dp % NY
    c, k = mem // 2, mem % 2

    def x_at(offset):
        return (dp, ((c + offset + NX) % NX) * 2 + k)

    others = [(2, 0), (2, 1), (1, 0), (-1, 0), (1, 1), (-1, 1), (0, 1)]

    def mem_peer(j):
        chips, cores = others[j - 1]
        return (dp, ((c + chips + NX) % NX) * 2 + (k + cores) % 2)

    def y_at(offset):
        return (z * NY + (y + offset) % NY, mem)

    def z_at(offset):
        return (((z + offset) % NZ) * NY + y, mem)

    sibling = (dp, mem + 1 - 2 * k)
    used = [0]
    pending = []

    def remote(src, dst, device):
        i = used[0]
        used[0] += 1
        return pltpu.make_async_remote_copy(
            src_ref=src,
            dst_ref=dst,
            send_sem=sems.at[0, i],
            recv_sem=sems.at[1, i],
            device_id=device,
            device_id_type=MESH,
        )

    def start(copies):
        for copy in copies:
            copy.start()
            pending.append(copy)

    def arrive(copies):
        for copy in copies:
            copy.wait_recv()

    def drain():
        while pending:
            pending.pop(0).wait_send()

    group = pl.ds(pl.multiple_of(z * 8, 8), 8)
    fetches = []
    for i in range(NS // KT):
        at = pl.ds(i * KT, KT)
        fetches.append(pltpu.make_async_copy(m_hbm.at[at], m_ref.at[at], loads.at[i]))
    for src, dst in (
        (cls_hbm, cls_ref),
        (obs_hbm, obs_ref),
        (var_hbm, var_ref),
        (ens_hbm.at[group], ensemble_in.at[mem]),
    ):
        fetches.append(pltpu.make_async_copy(src, dst, loads.at[len(fetches)]))
    for fetch in fetches:
        fetch.start()

    barrier = pltpu.get_barrier_semaphore()
    greeted = (
        [mem_peer(j) for j in range(1, NM)]
        + [y_at(j) for j in range(1, NY)]
        + [z_at(j) for j in range(1, NZ)]
    )
    for device in greeted:
        pl.semaphore_signal(barrier, inc=1, device_id=device, device_id_type=MESH)

    eye = (
        lax.broadcasted_iota(jnp.int32, (CM, CM), 0) == lax.broadcasted_iota(jnp.int32, (CM, CM), 1)
    )
    turn = jnp.concatenate(
        [jnp.where(eye, 1.0, 0.0), jnp.ones((16, CM), jnp.float32)], axis=0
    ).astype(jnp.bfloat16)
    for i in range(NS // KT):
        at = pl.ds(i * KT, KT)
        fetches[i].wait()
        turned = lax.dot_general(turn, m_ref[at, :], NT, preferred_element_type=jnp.float32)
        raw[:, at] = turned[:CM].astype(jnp.bfloat16)
        sums[mem, :, at] = turned[CM : CM + 1]
    for fetch in fetches[NS // KT :]:
        fetch.wait()

    pl.semaphore_wait(barrier, len(greeted))

    own = pl.ds(pl.multiple_of(k * CM, CM), CM)
    other = pl.ds(pl.multiple_of((1 - k) * CM, CM), CM)
    sum_copies = [remote(sums.at[mem], sums.at[mem], mem_peer(j)) for j in range(1, NM)]
    start(sum_copies)
    ens_copies = [
        remote(ensemble_in.at[mem], ensemble_in.at[mem], mem_peer(j)) for j in range(1, NM)
    ]
    start(ens_copies)
    sib_copy = remote(raw, sib, sibling)
    start([sib_copy])
    near_copies = []
    for first, count in zip(STARTS, CHUNKS, strict=True):
        at = pl.ds(first, count)
        near_copies.append(remote(raw.at[at], near.at[at], x_at(-1)))
    next_half = pl.multiple_of((((c + 1) % NX) // 2) * HALF, HALF)
    prev_copies, shared_copies = [], []
    for i in range(PREV):
        rows = CM // PREV
        to_rows = pl.ds(pl.multiple_of(k * CM + i * rows, rows), rows)
        prev_copies.append(
            remote(
                raw.at[pl.ds(i * rows, rows), pl.ds(next_half, HALF)], prev.at[to_rows], x_at(1)
            )
        )
        shared_copies.append(remote(prev.at[to_rows], prev.at[to_rows], sibling))
    start(near_copies)
    start(prev_copies)

    classes = cls_ref[...]
    variance = jnp.zeros((1, NS), jnp.float32)
    for level in range(8):
        variance = jnp.where(classes == level, var_ref[level], variance)
    weight = lax.rsqrt(variance)
    scale[...] = weight / math.sqrt(MEMBERS - 1)

    arrive(sum_copies)
    total = sums[0]
    for j in range(1, NM):
        total = total + sums[j]
    average = total / MEMBERS
    bases[...] = average
    innovation = weight * (obs_ref[...] - average)

    def whiten(block, at):
        return ((block.astype(jnp.float32) - bases[:, at]) * scale[:, at]).astype(jnp.bfloat16)

    for i in range(NS // KT):
        at = pl.ds(i * KT, KT)
        white[own, at] = whiten(raw[:, at], at)
    arrive([sib_copy])

    @pl.loop(0, NS // KT)
    def _(i):
        at = pl.ds(pl.multiple_of(i * KT, KT), KT)
        white[other, at] = whiten(sib[:, at], at)

    def reduce_y(q, _):
        gram_part(q)
        quarter = ROWS[q] // 4
        copies = []
        for j in range(1, NY):
            target = (y + j) % NY
            rows = pl.ds(pl.multiple_of(target * quarter, 8), quarter)
            copies.append(remote(part[q].at[rows], from_y[q].at[j - 1], y_at(j)))
        start(copies)
        return copies

    def reduce_z(q, copies):
        quarter = ROWS[q] // 4
        arrive(copies)
        mine = pl.ds(pl.multiple_of(y * quarter, 8), quarter)
        sum_y[q][...] = part[q][mine, :] + from_y[q][0] + from_y[q][1] + from_y[q][2]
        copies = []
        for j in FAR_Z:
            rows, lanes = piece(ROWS[q], (z + j) % NZ)
            copies.append(remote(sum_y[q].at[rows, lanes], from_z[q].at[j - 1], z_at(j)))
        start(copies)
        return copies

    def spread_z(q, copies):
        arrive(copies)
        rows, lanes = piece(ROWS[q], z)
        total = sum_y[q][rows, lanes]
        for j in range(NZ - 1):
            total = total + from_z[q][j]
        gather_z[q][rows, lanes] = total
        here = gather_z[q].at[rows, lanes]
        copies = [remote(here, here, z_at(j)) for j in FAR_Z]
        start(copies)
        return copies

    def spread_y(q, copies):
        quarter = ROWS[q] // 4
        arrive(copies)
        blocks, first_row, count, _ = PARTS[q]
        if len(blocks) == 1:
            first = blocks[0] * CM + first_row + y * quarter
        else:
            first = (blocks[0] + y // 2) * CM + first_row + (y % 2) * quarter
        rows = pl.ds(pl.multiple_of(first, 8), quarter)
        strip[rows, :] = gather_z[q][...]
        copies = [remote(gather_z[q], strip.at[rows], y_at(j)) for j in range(1, NY)]
        start(copies)
        return copies

    def finish(q, copies):
        arrive(copies)
        blocks, first_row, count, _ = PARTS[q]
        for block in blocks:
            at = pl.ds(block * CM + first_row, count)
            for i, term in enumerate(split_in_three(strip[at, :])):
                terms[i, at, :] = term

    half = pl.multiple_of((c // 2) * HALF, HALF)

    here_now = [0]

    def gram_part(q):
        blocks, first, count, needed = PARTS[q]
        while here_now[0] < needed:
            arrive([near_copies[here_now[0]]])
            here_now[0] += 1
        part[q][...] = jnp.zeros((ROWS[q], 512), jnp.float32)
        for place, block in enumerate(blocks):
            to = pl.ds(place * count, count)
            if block == 0:
                rows = pl.ds(pl.multiple_of(k * CM + first, 128), count)
            else:
                rows = pl.ds(first, count)

            @pl.loop(0, (HALF if block == 2 else NS) // KT)
            def _(s):
                here = pl.ds(pl.multiple_of(s * KT, KT), KT)
                if block == 0:
                    left, right = white[rows, here], white[:, here]
                elif block == 1:
                    left, right = whiten(near[rows, here], here), white[:, here]
                else:
                    at = pl.ds(pl.multiple_of(half + s * KT, KT), KT)
                    left, right = whiten(near[rows, at], at), white_prev[:, here]
                part[q][to] += lax.dot_general(left, right, NT, preferred_element_type=jnp.float32)

    def small_sums(_):
        shadow = lax.dot_general(
            stacked(innovation, 16), white[own, :], NT, preferred_element_type=jnp.float32
        )
        mine = pl.ds(pl.multiple_of(k * CM, CM), CM)
        square = jnp.concatenate([part[0][:, mine], part[1][:, mine]], axis=0)
        diagonal = jnp.sum(jnp.where(eye, square, 0.0), axis=0, keepdims=True)
        small[...] = jnp.concatenate(
            [jnp.sum(shadow[:8], axis=0, keepdims=True), diagonal, jnp.zeros((6, CM), jnp.float32)],
            axis=0,
        )
        copies = [remote(small, small_y.at[j - 1], y_at(j)) for j in range(1, NY)]
        start(copies)
        return copies

    def small_sum_y(copies):
        arrive(copies)
        small_z[NZ - 1] = small[...] + small_y[0] + small_y[1] + small_y[2]
        copies = [remote(small_z.at[NZ - 1], small_z.at[j - 1], z_at(j)) for j in FAR_Z]
        start(copies)
        return copies

    def small_sum_z(copies):
        arrive(copies)
        total = small_z[0]
        for j in range(1, NZ):
            total = total + small_z[j]
        small_m[mem] = total
        copies = [remote(small_m.at[mem], small_m.at[mem], mem_peer(j)) for j in range(1, NM)]
        start(copies)
        return copies

    def first_vectors(copies):
        arrive(ens_copies)
        arrive(copies)
        center = ensemble_in[0].sum(axis=1, keepdims=True)
        for j in range(1, NM):
            center = center + ensemble_in[j].sum(axis=1, keepdims=True)
        center = center / MEMBERS
        place = lax.broadcasted_iota(jnp.int32, (8, 1), 0)

        def own_rows(block):
            return [
                jnp.sum(jnp.where(place == 2 * y + i, block, 0.0), axis=0, keepdims=True)
                for i in range(2)
            ]

        centers[:2, :] = jnp.concatenate(own_rows(jnp.broadcast_to(center, (8, 128))), axis=0)
        for j in range(NM):
            vec[j] = jnp.concatenate(
                own_rows(ensemble_in[j] - center)
                + [small_m[j, 0:1, :], jnp.zeros((VR - 3, CM), jnp.float32)],
                axis=0,
            )

    def share_prev(i):
        arrive([prev_copies[i]])
        start([shared_copies[i]])

    def whiten_prev():
        arrive(shared_copies)

        @pl.loop(0, HALF // KT)
        def _(s):
            here = pl.ds(pl.multiple_of(s * KT, KT), KT)
            at = pl.ds(pl.multiple_of(half + s * KT, KT), KT)
            white_prev[:, here] = whiten(prev[:, here], at)

    stages = (reduce_y, reduce_z, spread_z, spread_y, finish)
    state = [None] * n
    small_state = None
    for item in ORDER:
        if item == "prev 0":
            share_prev(0)
        elif item == "prev 1":
            share_prev(1)
        elif item == "white prev":
            whiten_prev()
        elif item == "small":
            small_state = small_sums(None)
        elif item == "small y":
            small_state = small_sum_y(small_state)
        elif item == "small z":
            small_state = small_sum_z(small_state)
        elif item == "vectors":
            first_vectors(small_state)
        else:
            q, stage = item
            state[q] = stages[stage](q, state[q])

    trace = small_m[0, 1:2, :]
    for j in range(1, NM):
        trace = trace + small_m[j, 1:2, :]
    norm = (MEMBERS + jnp.sum(trace, axis=1, keepdims=True)) / MEMBERS

    def folded(rows):
        return rows[:VR] + rows[VR : 2 * VR] + rows[2 * VR : 3 * VR]

    def times(step):
        ahead = vec[((c + 1) % NX) * 2 + k]
        behind = ((c + NX - 1) % NX) * 2
        down = stacked(jnp.concatenate([vec[mem], ahead], axis=1), 4 * VR)
        across = stacked(jnp.concatenate([vec[2 * c], vec[2 * c + 1]], axis=1), 4 * VR)
        back = stacked(jnp.concatenate([vec[behind], vec[behind + 1]], axis=1), 4 * VR)
        for_next = for_own = for_last = 0.0
        for i in range(3):
            for_next = (
                for_next
                + lax.dot_general(
                    across, terms[i, CM : 2 * CM, :], NT, preferred_element_type=jnp.float32
                )
                + lax.dot_general(
                    back, terms[i, 2 * CM :, :], NT, preferred_element_type=jnp.float32
                )
            )
            for_own = for_own + jnp.dot(
                down, terms[i, : 2 * CM, :], preferred_element_type=jnp.float32
            )
            for_last = for_last + jnp.dot(
                down[:, CM:], terms[i, 2 * CM :, :], preferred_element_type=jnp.float32
            )
        exchange[step, mem, :, :CM] = folded(for_next)
        exchange[step, mem, :, CM : 3 * CM] = folded(for_own)
        exchange[step, mem, :, 3 * CM :] = folded(for_last)
        here = exchange.at[step, mem]
        copies = [remote(here, here, mem_peer(j)) for j in range(1, NM)]
        start(copies)
        arrive(copies)
        result = []
        for chip in range(NX):
            for core in range(2):
                mine = slice((core + 1) * CM, (core + 2) * CM)
                last = slice((core + 3) * CM, (core + 4) * CM)
                above = 2 * ((chip + 1) % NX)
                product = (
                    exchange[step, 2 * ((chip - 1) % NX) + core, :, :CM]
                    + exchange[step, 2 * chip, :, mine]
                    + exchange[step, 2 * chip + 1, :, mine]
                    + exchange[step, above, :, last]
                    + exchange[step, above + 1, :, last]
                )
                result.append((product + vec[2 * chip + core]) / norm)
        return result

    moved = times(0)
    for j in range(NM):
        vec[j] = 1.5 * vec[j] - 0.5 * moved[j]
        polys[j] = vec[j]
    moved = times(1)
    for j in range(NM):
        vec[j] = 1.5 * vec[j] - 0.5 * moved[j]
    moved = times(2)
    for j in range(NM):
        vec[j] = moved[j]
    moved = times(3)
    shift = jnp.zeros((2, 1), jnp.float32)
    for j in range(NM):
        applied = 1.5 * polys[j] - 0.5 * (1.5 * vec[j] - 0.5 * moved[j])
        polys[j] = applied
        shift = shift + jnp.sum(applied[:2] * applied[2:3], axis=1, keepdims=True)
    shift = shift / norm / math.sqrt(MEMBERS - 1)
    rows_out[y, :2, :] = centers[:2, :1] + shift + polys[mem][:2] / jnp.sqrt(norm)
    here = rows_out.at[y]
    copies = [remote(here, here, y_at(j)) for j in range(1, NY)]
    start(copies)
    arrive(copies)
    out_ref[group, :] = jnp.concatenate([rows_out[j, :2, :] for j in range(NY)], axis=0)
    here = out_ref.at[group]
    copies = [remote(here, here, z_at(j)) for j in FAR_Z]
    start(copies)
    arrive(copies)
    drain()


def shards(modelled_reactions, observations, noise_class, class_variance, ensemble):
    f32, bf16 = jnp.float32, jnp.bfloat16
    hbm = pl.BlockSpec(memory_space=pltpu.HBM)
    scratch = [
        pltpu.VMEM((NS, CM), bf16),
        pltpu.VMEM((1, NS), f32),
        pltpu.VMEM((1, NS), jnp.int32),
        pltpu.SMEM((8,), f32),
        pltpu.VMEM((CM, NS), bf16),
        pltpu.VMEM((CM, NS), bf16),
        pltpu.VMEM((2 * CM, HALF), bf16),
        pltpu.VMEM((CM, NS), bf16),
        pltpu.VMEM((2 * CM, NS), bf16),
        pltpu.VMEM((2 * CM, HALF), bf16),
        pltpu.VMEM((NM, 1, NS), f32),
        pltpu.VMEM((1, NS), f32),
        pltpu.VMEM((1, NS), f32),
        pltpu.VMEM((NM, 8, CM), f32),
        pltpu.VMEM((8, 128), f32),
        pltpu.VMEM((8, CM), f32),
        pltpu.VMEM((NY - 1, 8, CM), f32),
        pltpu.VMEM((NZ, 8, CM), f32),
        pltpu.VMEM((NM, 8, CM), f32),
        pltpu.VMEM((3 * CM, 512), f32),
        pltpu.VMEM((3, 3 * CM, 512), bf16),
        pltpu.VMEM((NM, VR, CM), f32),
        pltpu.VMEM((NM, VR, CM), f32),
        pltpu.VMEM((4, NM, VR, WIDE), f32),
        pltpu.VMEM((NY, 8, CM), f32),
        pltpu.SemaphoreType.DMA((N_LOADS,)),
        pltpu.SemaphoreType.DMA((2, N_SEMS)),
    ]
    scratch += [pltpu.VMEM((r, 512), f32) for r in ROWS]
    scratch += [pltpu.VMEM((NY - 1, r // 4, 512), f32) for r in ROWS]
    scratch += [pltpu.VMEM((r // 4, 512), f32) for r in ROWS]
    scratch += [pltpu.VMEM((NZ - 1,) + piece_shape(r), f32) for r in ROWS]
    scratch += [pltpu.VMEM((r // 4, 512), f32) for r in ROWS]
    return pl.pallas_call(
        kernel,
        out_shape=jax.ShapeDtypeStruct((64, CM), f32),
        in_specs=[hbm] * 5,
        out_specs=pl.BlockSpec(memory_space=pltpu.VMEM),
        scratch_shapes=scratch,
        compiler_params=pltpu.CompilerParams(
            collective_id=0, has_side_effects=True, vmem_limit_bytes=60 * 1024 * 1024
        ),
    )(
        class_variance,
        modelled_reactions,
        observations.reshape(1, NS),
        noise_class.reshape(1, NS),
        ensemble,
    )


def solution(mesh):
    placed = (P("dp", "mem"), P("dp"), P("dp"), P(), P(None, "mem"))
    return jax.shard_map(
        shards, mesh=mesh, in_specs=placed, out_specs=P(None, "mem"), check_vma=False
    )
```

```python
import math

import jax
import jax.numpy as jnp
from jax import lax
from jax.experimental import pallas as pl
from jax.experimental.pallas import tpu as pltpu
from jax.sharding import PartitionSpec as P

MESH = pl.DeviceIdType.MESH
NX, NY, NZ, NM = 4, 4, 8, 8
MEMBERS = 2048
CM = 256
NS = 3072
HALF = NS // 2
KT = 512
CHUNKS = (64, 64, 64, 32, 32)
STARTS = tuple(sum(CHUNKS[:i]) for i in range(len(CHUNKS)))
PARTS = (
    ((0,), 0, 128, 0),
    ((0,), 128, 128, 0),
    ((1,), 0, 64, 1),
    ((1,), 64, 64, 2),
    ((2,), 0, 128, 2),
    ((1, 2), 128, 64, 3),
    ((1, 2), 192, 32, 4),
    ((1, 2), 224, 32, 5),
)
ROWS = tuple(len(blocks) * count for blocks, _, count, _ in PARTS)
ORDER = (
    (0, 0), (1, 0), "small", (2, 0), "prev 0", (2, 1), (0, 1), (1, 1), "prev 1", (3, 0), "white prev", (4, 0),
    (2, 2), "small y", (3, 1), (1, 2), (5, 0), (0, 2), (4, 1), (3, 2), "small z", (1, 3), (6, 0), (5, 1), (7, 0),
    (0, 3), (4, 2), (6, 1), (2, 3), (3, 3), (7, 1), (5, 2), (4, 3), (6, 2), (7, 2), (5, 3), (1, 4), (6, 3),
    "vectors", (7, 3), (0, 4), (4, 4), (6, 4), (5, 4), (3, 4), (2, 4), (7, 4),
)
PREV = 2
VR = 4
WIDE = 5 * CM
N_SEMS = 4 * len(ROWS) + len(CHUNKS) + 2 * PREV + 15
N_LOADS = NS // KT + 4
FAR_Z = (4, 3, 5, 2, 6, 1, 7)
NT = (((1,), (1,)), ((), ()))


def piece(rows, index):
    groups = rows // 4 // 8
    lanes = NZ // groups
    width = 512 // lanes
    return (
        pl.ds(pl.multiple_of((index // lanes) * 8, 8), 8),
        pl.ds(pl.multiple_of((index % lanes) * width, 128), width),
    )


def piece_shape(rows):
    return (8, 512 // (NZ // (rows // 4 // 8)))


def split_in_three(value):
    high = value.astype(jnp.bfloat16)
    rest = value - high.astype(jnp.float32)
    middle = rest.astype(jnp.bfloat16)
    return high, middle, (rest - middle.astype(jnp.float32)).astype(jnp.bfloat16)


def stacked(value, rows):
    terms = [term.astype(jnp.float32) for term in split_in_three(value)]
    spare = rows - 3 * value.shape[0]
    return jnp.concatenate(
        terms + [jnp.zeros((spare, value.shape[1]), jnp.float32)], axis=0
    ).astype(jnp.bfloat16)


def kernel(var_hbm, m_hbm, obs_hbm, cls_hbm, ens_hbm, out_ref, *scratch):
    (
        m_ref, obs_ref, cls_ref, var_ref, raw, near, prev, sib, white, white_prev, sums, scale, bases,
        ensemble_in, centers, small, small_y, small_z, small_m, strip, terms, vec, polys, exchange,
        rows_out, loads, sems,
    ) = scratch[:27]
    lists = scratch[27:]
    n = len(ROWS)
    part, from_y, sum_y, from_z, gather_z = (lists[i * n : (i + 1) * n] for i in range(5))

    dp, mem = lax.axis_index("dp"), lax.axis_index("mem")
    z, y = dp // NY, dp % NY
    c, k = mem // 2, mem % 2

    def x_at(offset):
        return (dp, ((c + offset + NX) % NX) * 2 + k)

    others = [(2, 0), (2, 1), (1, 0), (-1, 0), (1, 1), (-1, 1), (0, 1)]

    def x_pair(chips, core):
        return (dp, ((c + chips + NX) % NX) * 2 + core)

    def mem_peer(j):
        chips, cores = others[j - 1]
        return x_pair(chips, (k + cores) % 2)

    def y_at(offset):
        return (z * NY + (y + offset) % NY, mem)

    def z_at(offset):
        return (((z + offset) % NZ) * NY + y, mem)

    sibling = (dp, mem + 1 - 2 * k)
    started = []

    def start(group, landing):
        i = len(started)
        for src, dst, device in group:
            pltpu.make_async_remote_copy(
                src_ref=src,
                dst_ref=dst,
                send_sem=sems.at[0, i],
                recv_sem=sems.at[1, i],
                device_id=device,
                device_id_type=MESH,
            ).start()
        started.append(landing)
        return i

    def arrive(i):
        pltpu.make_async_copy(started[i], started[i], sems.at[1, i]).wait()

    def drain():
        for i, landing in enumerate(started):
            pltpu.make_async_copy(landing, landing, sems.at[0, i]).wait()

    group = pl.ds(pl.multiple_of(z * 8, 8), 8)
    fetches = []
    for i in range(NS // KT):
        at = pl.ds(i * KT, KT)
        fetches.append(pltpu.make_async_copy(m_hbm.at[at], m_ref.at[at], loads.at[i]))
    for src, dst in (
        (cls_hbm, cls_ref),
        (obs_hbm, obs_ref),
        (var_hbm, var_ref),
        (ens_hbm.at[group], ensemble_in.at[mem]),
    ):
        fetches.append(pltpu.make_async_copy(src, dst, loads.at[len(fetches)]))
    for fetch in fetches:
        fetch.start()

    barrier = pltpu.get_barrier_semaphore()
    greeted = (
        [mem_peer(j) for j in range(1, NM)]
        + [y_at(j) for j in range(1, NY)]
        + [z_at(j) for j in range(1, NZ)]
    )
    for device in greeted:
        pl.semaphore_signal(barrier, inc=1, device_id=device, device_id_type=MESH)

    eye = (
        lax.broadcasted_iota(jnp.int32, (CM, CM), 0) == lax.broadcasted_iota(jnp.int32, (CM, CM), 1)
    )
    turn = jnp.concatenate(
        [jnp.where(eye, 1.0, 0.0), jnp.ones((16, CM), jnp.float32)], axis=0
    ).astype(jnp.bfloat16)
    for i in range(NS // KT):
        at = pl.ds(i * KT, KT)
        fetches[i].wait()
        turned = lax.dot_general(turn, m_ref[at, :], NT, preferred_element_type=jnp.float32)
        raw[:, at] = turned[:CM].astype(jnp.bfloat16)
        sums[mem, :, at] = turned[CM : CM + 1]
    for fetch in fetches[NS // KT :]:
        fetch.wait()

    pl.semaphore_wait(barrier, len(greeted))

    own = pl.ds(pl.multiple_of(k * CM, CM), CM)
    other = pl.ds(pl.multiple_of((1 - k) * CM, CM), CM)
    first_seven = pl.ds(0, NM - 1)

    def to_mem(here, landing):
        return start([(here, here, mem_peer(j)) for j in range(1, NM)], landing)

    sum_copies = to_mem(sums.at[mem], sums.at[first_seven])
    ens_copies = to_mem(ensemble_in.at[mem], ensemble_in.at[first_seven])
    sib_copy = start([(raw, sib, sibling)], raw)
    near_copies = []
    for first, count in zip(STARTS, CHUNKS, strict=True):
        at = pl.ds(first, count)
        near_copies.append(start([(raw.at[at], near.at[at], x_at(-1))], raw.at[at]))
    next_half = pl.multiple_of((((c + 1) % NX) // 2) * HALF, HALF)
    prev_rows = [
        pl.ds(pl.multiple_of(k * CM + i * (CM // PREV), CM // PREV), CM // PREV) for i in range(PREV)
    ]
    prev_copies, shared_copies = [], []
    for i, to_rows in enumerate(prev_rows):
        src = raw.at[pl.ds(i * (CM // PREV), CM // PREV), pl.ds(next_half, HALF)]
        prev_copies.append(start([(src, prev.at[to_rows], x_at(1))], prev.at[to_rows]))

    classes = cls_ref[...]
    variance = jnp.zeros((1, NS), jnp.float32)
    for level in range(8):
        variance = jnp.where(classes == level, var_ref[level], variance)
    weight = lax.rsqrt(variance)
    scale[...] = weight / math.sqrt(MEMBERS - 1)

    arrive(sum_copies)
    total = sums[0]
    for j in range(1, NM):
        total = total + sums[j]
    average = total / MEMBERS
    bases[...] = average
    innovation = weight * (obs_ref[...] - average)

    def whiten(block, at):
        return ((block.astype(jnp.float32) - bases[:, at]) * scale[:, at]).astype(jnp.bfloat16)

    for i in range(NS // KT):
        at = pl.ds(i * KT, KT)
        white[own, at] = whiten(raw[:, at], at)
    arrive(sib_copy)

    @pl.loop(0, NS // KT)
    def _(i):
        at = pl.ds(pl.multiple_of(i * KT, KT), KT)
        white[other, at] = whiten(sib[:, at], at)

    def reduce_y(q, _):
        gram_part(q)
        quarter = ROWS[q] // 4
        group = []
        for j in range(1, NY):
            target = (y + j) % NY
            rows = pl.ds(pl.multiple_of(target * quarter, 8), quarter)
            group.append((part[q].at[rows], from_y[q].at[j - 1], y_at(j)))
        return start(group, from_y[q])

    def reduce_z(q, copies):
        quarter = ROWS[q] // 4
        arrive(copies)
        mine = pl.ds(pl.multiple_of(y * quarter, 8), quarter)
        sum_y[q][...] = part[q][mine, :] + from_y[q][0] + from_y[q][1] + from_y[q][2]
        group = []
        for j in FAR_Z:
            rows, lanes = piece(ROWS[q], (z + j) % NZ)
            group.append((sum_y[q].at[rows, lanes], from_z[q].at[j - 1], z_at(j)))
        return start(group, from_z[q])

    def spread_z(q, copies):
        arrive(copies)
        rows, lanes = piece(ROWS[q], z)
        total = sum_y[q][rows, lanes]
        for j in range(NZ - 1):
            total = total + from_z[q][j]
        gather_z[q][rows, lanes] = total
        here = gather_z[q].at[rows, lanes]
        return start([(here, here, z_at(j)) for j in FAR_Z], from_z[q])

    def spread_y(q, copies):
        quarter = ROWS[q] // 4
        arrive(copies)
        blocks, first_row, count, _ = PARTS[q]
        if len(blocks) == 1:
            first = blocks[0] * CM + first_row + y * quarter
        else:
            first = (blocks[0] + y // 2) * CM + first_row + (y % 2) * quarter
        rows = pl.ds(pl.multiple_of(first, 8), quarter)
        strip[rows, :] = gather_z[q][...]
        return start([(gather_z[q], strip.at[rows], y_at(j)) for j in range(1, NY)], from_y[q])

    def finish(q, copies):
        arrive(copies)
        blocks, first_row, count, _ = PARTS[q]
        for block in blocks:
            at = pl.ds(block * CM + first_row, count)
            for i, term in enumerate(split_in_three(strip[at, :])):
                terms[i, at, :] = term

    half = pl.multiple_of((c // 2) * HALF, HALF)

    here_now = [0]

    def gram_part(q):
        blocks, first, count, needed = PARTS[q]
        while here_now[0] < needed:
            arrive(near_copies[here_now[0]])
            here_now[0] += 1
        part[q][...] = jnp.zeros((ROWS[q], 512), jnp.float32)
        for place, block in enumerate(blocks):
            to = pl.ds(place * count, count)
            if block == 0:
                rows = pl.ds(pl.multiple_of(k * CM + first, 128), count)
            else:
                rows = pl.ds(first, count)

            @pl.loop(0, (HALF if block == 2 else NS) // KT)
            def _(s):
                here = pl.ds(pl.multiple_of(s * KT, KT), KT)
                if block == 0:
                    left, right = white[rows, here], white[:, here]
                elif block == 1:
                    left, right = whiten(near[rows, here], here), white[:, here]
                else:
                    at = pl.ds(pl.multiple_of(half + s * KT, KT), KT)
                    left, right = whiten(near[rows, at], at), white_prev[:, here]
                part[q][to] += lax.dot_general(left, right, NT, preferred_element_type=jnp.float32)

    def small_sums(_):
        shadow = lax.dot_general(
            stacked(innovation, 16), white[own, :], NT, preferred_element_type=jnp.float32
        )
        mine = pl.ds(pl.multiple_of(k * CM, CM), CM)
        square = jnp.concatenate([part[0][:, mine], part[1][:, mine]], axis=0)
        diagonal = jnp.sum(jnp.where(eye, square, 0.0), axis=0, keepdims=True)
        small[...] = jnp.concatenate(
            [jnp.sum(shadow[:8], axis=0, keepdims=True), diagonal, jnp.zeros((6, CM), jnp.float32)],
            axis=0,
        )
        return start([(small, small_y.at[j - 1], y_at(j)) for j in range(1, NY)], small_y)

    def small_sum_y(copies):
        arrive(copies)
        small_z[NZ - 1] = small[...] + small_y[0] + small_y[1] + small_y[2]
        return start(
            [(small_z.at[NZ - 1], small_z.at[j - 1], z_at(j)) for j in FAR_Z], small_z.at[first_seven]
        )

    def small_sum_z(copies):
        arrive(copies)
        total = small_z[0]
        for j in range(1, NZ):
            total = total + small_z[j]
        small_m[mem] = total
        return to_mem(small_m.at[mem], small_m.at[first_seven])

    def first_vectors(copies):
        arrive(ens_copies)
        arrive(copies)
        center = ensemble_in[0].sum(axis=1, keepdims=True)
        for j in range(1, NM):
            center = center + ensemble_in[j].sum(axis=1, keepdims=True)
        center = center / MEMBERS
        place = lax.broadcasted_iota(jnp.int32, (8, 1), 0)

        def own_rows(block):
            return [
                jnp.sum(jnp.where(place == 2 * y + i, block, 0.0), axis=0, keepdims=True)
                for i in range(2)
            ]

        centers[:2, :] = jnp.concatenate(own_rows(jnp.broadcast_to(center, (8, 128))), axis=0)
        for j in range(NM):
            vec[j] = jnp.concatenate(
                own_rows(ensemble_in[j] - center)
                + [small_m[j, 0:1, :], jnp.zeros((VR - 3, CM), jnp.float32)],
                axis=0,
            )

    def share_prev(i):
        arrive(prev_copies[i])
        rows = prev.at[prev_rows[i]]
        shared_copies.append(start([(rows, rows, sibling)], rows))

    def whiten_prev():
        for copies in shared_copies:
            arrive(copies)

        @pl.loop(0, HALF // KT)
        def _(s):
            here = pl.ds(pl.multiple_of(s * KT, KT), KT)
            at = pl.ds(pl.multiple_of(half + s * KT, KT), KT)
            white_prev[:, here] = whiten(prev[:, here], at)

    stages = (reduce_y, reduce_z, spread_z, spread_y, finish)
    state = [None] * n
    small_state = None
    for item in ORDER:
        if item == "prev 0":
            share_prev(0)
        elif item == "prev 1":
            share_prev(1)
        elif item == "white prev":
            whiten_prev()
        elif item == "small":
            small_state = small_sums(None)
        elif item == "small y":
            small_state = small_sum_y(small_state)
        elif item == "small z":
            small_state = small_sum_z(small_state)
        elif item == "vectors":
            first_vectors(small_state)
        else:
            q, stage = item
            state[q] = stages[stage](q, state[q])

    trace = small_m[0, 1:2, :]
    for j in range(1, NM):
        trace = trace + small_m[j, 1:2, :]
    norm = (MEMBERS + jnp.sum(trace, axis=1, keepdims=True)) / MEMBERS

    def folded(rows):
        return rows[:VR] + rows[VR : 2 * VR] + rows[2 * VR : 3 * VR]

    def times(step):
        ahead = vec[((c + 1) % NX) * 2 + k]
        behind = ((c + NX - 1) % NX) * 2
        down = stacked(jnp.concatenate([vec[mem], ahead], axis=1), 4 * VR)
        across = stacked(jnp.concatenate([vec[2 * c], vec[2 * c + 1]], axis=1), 4 * VR)
        back = stacked(jnp.concatenate([vec[behind], vec[behind + 1]], axis=1), 4 * VR)
        for_next = for_own = for_last = 0.0
        for i in range(3):
            for_next = (
                for_next
                + lax.dot_general(
                    across, terms[i, CM : 2 * CM, :], NT, preferred_element_type=jnp.float32
                )
                + lax.dot_general(
                    back, terms[i, 2 * CM :, :], NT, preferred_element_type=jnp.float32
                )
            )
            for_own = for_own + jnp.dot(
                down, terms[i, : 2 * CM, :], preferred_element_type=jnp.float32
            )
            for_last = for_last + jnp.dot(
                down[:, CM:], terms[i, 2 * CM :, :], preferred_element_type=jnp.float32
            )
        exchange[step, mem, :, :CM] = folded(for_next)
        exchange[step, mem, :, CM : 3 * CM] = folded(for_own)
        mine = pl.ds(pl.multiple_of((k + 1) * CM, CM), CM)
        exchange[step, mem, :, mine] += vec[mem]
        exchange[step, mem, :, 3 * CM :] = folded(for_last)
        def block(lanes):
            return exchange.at[step, mem, :, lanes]

        def landing(count, lanes):
            return exchange.at[step, pl.ds(0, count), :, pl.ds(0, lanes)]

        if step == 1:
            across_ring = [x_pair(2, core) for core in range(2)]
            far = [(block(pl.ds(0, CM)),) * 2 + (device,) for device in across_ring]
            for core, device in enumerate(across_ring):
                lanes = pl.ds((3 + core) * CM, CM)
                far.append((block(lanes), block(lanes), device))
            ahead_part, rest = block(pl.ds(0, 3 * CM)), block(pl.ds(CM, 4 * CM))
            groups = [
                start(far, landing(4, CM)),
                start([(ahead_part, ahead_part, x_pair(1, core)) for core in range(2)], landing(2, 3 * CM)),
                start([(rest, rest, x_pair(-1, core)) for core in range(2)], landing(2, 4 * CM)),
                start([(rest, rest, sibling)], landing(1, 4 * CM)),
            ]
        else:
            groups = [to_mem(exchange.at[step, mem], exchange.at[step, first_seven])]
        for copies in groups:
            arrive(copies)

    def product(step, chip, core):
        mine = pl.ds(pl.multiple_of((core + 1) * CM, CM), CM)
        last = pl.ds(pl.multiple_of((core + 3) * CM, CM), CM)
        below, above = 2 * ((chip + NX - 1) % NX), 2 * ((chip + 1) % NX)
        at = 2 * chip
        whole = (
            exchange[step, below + core, :, pl.ds(0, CM)]
            + exchange[step, at, :, mine]
            + exchange[step, at + 1, :, mine]
            + exchange[step, above, :, last]
            + exchange[step, above + 1, :, last]
        )
        return whole / norm

    everyone = [(chip, core) for chip in range(NX) for core in range(2)]
    neighbours = [(c, 0), (c, 1), ((c + 1) % NX, k), ((c + NX - 1) % NX, 0), ((c + NX - 1) % NX, 1)]

    def apply(step, pieces, update):
        times(step)
        moved = [product(step, chip, core) for chip, core in pieces]
        for (chip, core), value in zip(pieces, moved, strict=True):
            at = 2 * chip + core
            vec[at] = update(vec[at], value)

    apply(0, everyone, lambda old, value: 1.5 * old - 0.5 * value)
    polys[...] = vec[...]
    apply(1, neighbours, lambda old, value: 1.5 * old - 0.5 * value)
    apply(2, everyone, lambda old, value: value)
    times(3)
    shift = jnp.zeros((2, 1), jnp.float32)
    for chip, core in everyone:
        at = 2 * chip + core
        applied = 1.5 * polys[at] - 0.5 * (1.5 * vec[at] - 0.5 * product(3, chip, core))
        polys[at] = applied
        shift = shift + jnp.sum(applied[:2] * applied[2:3], axis=1, keepdims=True)
    shift = shift / norm / math.sqrt(MEMBERS - 1)
    rows_out[y, :2, :] = centers[:2, :1] + shift + polys[mem][:2] / jnp.sqrt(norm)
    here = rows_out.at[y]
    arrive(start([(here, here, y_at(j)) for j in range(1, NY)], rows_out.at[pl.ds(0, NY - 1)]))
    out_ref[group, :] = jnp.concatenate([rows_out[j, :2, :] for j in range(NY)], axis=0)
    here = out_ref.at[group]
    arrive(start([(here, here, z_at(j)) for j in FAR_Z], out_ref.at[pl.ds(0, 8 * (NZ - 1))]))
    drain()


def shards(modelled_reactions, observations, noise_class, class_variance, ensemble):
    f32, bf16 = jnp.float32, jnp.bfloat16
    hbm = pl.BlockSpec(memory_space=pltpu.HBM)
    scratch = [
        pltpu.VMEM((NS, CM), bf16),
        pltpu.VMEM((1, NS), f32),
        pltpu.VMEM((1, NS), jnp.int32),
        pltpu.SMEM((8,), f32),
        pltpu.VMEM((CM, NS), bf16),
        pltpu.VMEM((CM, NS), bf16),
        pltpu.VMEM((2 * CM, HALF), bf16),
        pltpu.VMEM((CM, NS), bf16),
        pltpu.VMEM((2 * CM, NS), bf16),
        pltpu.VMEM((2 * CM, HALF), bf16),
        pltpu.VMEM((NM, 1, NS), f32),
        pltpu.VMEM((1, NS), f32),
        pltpu.VMEM((1, NS), f32),
        pltpu.VMEM((NM, 8, CM), f32),
        pltpu.VMEM((8, 128), f32),
        pltpu.VMEM((8, CM), f32),
        pltpu.VMEM((NY - 1, 8, CM), f32),
        pltpu.VMEM((NZ, 8, CM), f32),
        pltpu.VMEM((NM, 8, CM), f32),
        pltpu.VMEM((3 * CM, 512), f32),
        pltpu.VMEM((3, 3 * CM, 512), bf16),
        pltpu.VMEM((NM, VR, CM), f32),
        pltpu.VMEM((NM, VR, CM), f32),
        pltpu.VMEM((4, NM, VR, WIDE), f32),
        pltpu.VMEM((NY, 8, CM), f32),
        pltpu.SemaphoreType.DMA((N_LOADS,)),
        pltpu.SemaphoreType.DMA((2, N_SEMS)),
    ]
    scratch += [pltpu.VMEM((r, 512), f32) for r in ROWS]
    scratch += [pltpu.VMEM((NY - 1, r // 4, 512), f32) for r in ROWS]
    scratch += [pltpu.VMEM((r // 4, 512), f32) for r in ROWS]
    scratch += [pltpu.VMEM((NZ - 1,) + piece_shape(r), f32) for r in ROWS]
    scratch += [pltpu.VMEM((r // 4, 512), f32) for r in ROWS]
    return pl.pallas_call(
        kernel,
        out_shape=jax.ShapeDtypeStruct((64, CM), f32),
        in_specs=[hbm] * 5,
        out_specs=pl.BlockSpec(memory_space=pltpu.VMEM),
        scratch_shapes=scratch,
        compiler_params=pltpu.CompilerParams(
            collective_id=0, has_side_effects=True, vmem_limit_bytes=60 * 1024 * 1024
        ),
    )(
        class_variance,
        modelled_reactions,
        observations.reshape(1, NS),
        noise_class.reshape(1, NS),
        ensemble,
    )


def solution(mesh):
    placed = (P("dp", "mem"), P("dp"), P("dp"), P(), P(None, "mem"))
    return jax.shard_map(
        shards, mesh=mesh, in_specs=placed, out_specs=P(None, "mem"), check_vma=False
    )
```

```python
import math

import jax
import jax.numpy as jnp
from jax import lax
from jax.experimental import pallas as pl
from jax.experimental.pallas import tpu as pltpu
from jax.sharding import PartitionSpec as P

MESH = pl.DeviceIdType.MESH
NX, NY, NZ, NM = 4, 4, 8, 8
MEMBERS = 2048
CM = 256
NS = 3072
HALF = NS // 2
KT = 512
CHUNKS = (64, 64, 64, 32, 32)
STARTS = tuple(sum(CHUNKS[:i]) for i in range(len(CHUNKS)))
PARTS = (
    ((0,), 0, 128, 0),
    ((0,), 128, 128, 0),
    ((1,), 0, 64, 1),
    ((1,), 64, 64, 2),
    ((2,), 0, 128, 2),
    ((1, 2), 128, 64, 3),
    ((1, 2), 192, 32, 4),
    ((1, 2), 224, 32, 5),
)
ROWS = tuple(len(blocks) * count for blocks, _, count, _ in PARTS)
ORDER = (
    (0, 0), (1, 0), "small", (2, 0), "prev 0", (2, 1), (0, 1), (1, 1), "prev 1", (3, 0), "white prev", (4, 0),
    (2, 2), "small y", (3, 1), (1, 2), (5, 0), (0, 2), (4, 1), (3, 2), "small z", (1, 3), (6, 0), (5, 1), (7, 0),
    (0, 3), (4, 2), (6, 1), (2, 3), (3, 3), (7, 1), (5, 2), (4, 3), (6, 2), (7, 2), (5, 3), (1, 4), (6, 3),
    "vectors", (7, 3), (0, 4), (4, 4), (6, 4), (5, 4), (3, 4), (2, 4), (7, 4),
)
PREV = 2
VR = 4
WIDE = 5 * CM
N_SEMS = 4 * len(ROWS) + len(CHUNKS) + 1 + PREV + 1 + 3 + 3 + 7 + 2
N_LOADS = NS // KT + 4
FAR_Z = (4, 3, 5, 2, 6, 1, 7)
NT = (((1,), (1,)), ((), ()))


def piece(rows, index):
    groups = rows // 4 // 8
    lanes = NZ // groups
    width = 512 // lanes
    return (
        pl.ds(pl.multiple_of((index // lanes) * 8, 8), 8),
        pl.ds(pl.multiple_of((index % lanes) * width, 128), width),
    )


def piece_shape(rows):
    return (8, 512 // (NZ // (rows // 4 // 8)))


def split_in_three(value):
    high = value.astype(jnp.bfloat16)
    rest = value - high.astype(jnp.float32)
    middle = rest.astype(jnp.bfloat16)
    return high, middle, (rest - middle.astype(jnp.float32)).astype(jnp.bfloat16)


def stacked(value, rows):
    terms = [term.astype(jnp.float32) for term in split_in_three(value)]
    spare = rows - 3 * value.shape[0]
    return jnp.concatenate(
        terms + [jnp.zeros((spare, value.shape[1]), jnp.float32)], axis=0
    ).astype(jnp.bfloat16)


def kernel(var_hbm, m_hbm, obs_hbm, cls_hbm, ens_hbm, out_ref, *scratch):
    (
        m_ref, obs_ref, cls_ref, var_ref, raw, near, prev, sib, white, white_prev, sums, scale, bases,
        ensemble_in, centers, small, small_y, small_z, small_m, strip, terms, vec, polys, exchange,
        rows_out, norms, tally, loads, sems,
    ) = scratch[:29]
    lists = scratch[29:]
    n = len(ROWS)
    part, from_y, sum_y, from_z, gather_z = (lists[i * n : (i + 1) * n] for i in range(5))

    dp, mem = lax.axis_index("dp"), lax.axis_index("mem")
    z, y = dp // NY, dp % NY
    c, k = mem // 2, mem % 2

    def x_at(offset):
        return (dp, ((c + offset + NX) % NX) * 2 + k)

    others = [(2, 0), (2, 1), (1, 0), (-1, 0), (1, 1), (-1, 1), (0, 1)]

    def x_pair(chips, core):
        return (dp, ((c + chips + NX) % NX) * 2 + core)

    def mem_peer(j):
        chips, cores = others[j - 1]
        return x_pair(chips, (k + cores) % 2)

    def y_at(offset):
        return (z * NY + (y + offset) % NY, mem)

    def z_at(offset):
        return (((z + offset) % NZ) * NY + y, mem)

    sibling = (dp, mem + 1 - 2 * k)
    started = []

    def start(group, landing, i=None):
        if i is None:
            i = len(started)
            started.append(landing)
        for src, dst, device in group:
            pltpu.make_async_remote_copy(
                src_ref=src,
                dst_ref=dst,
                send_sem=sems.at[0, i],
                recv_sem=sems.at[1, i],
                device_id=device,
                device_id_type=MESH,
            ).start()
        return i

    def arrive(i):
        pltpu.make_async_copy(started[i], started[i], sems.at[1, i]).wait()

    def drain():
        for i, landing in enumerate(started):
            pltpu.make_async_copy(landing, landing, sems.at[0, i]).wait()

    group = pl.ds(pl.multiple_of(z * 8, 8), 8)
    fetches = []
    for i in range(NS // KT):
        at = pl.ds(i * KT, KT)
        fetches.append(pltpu.make_async_copy(m_hbm.at[at], m_ref.at[at], loads.at[i]))
    for src, dst in (
        (cls_hbm, cls_ref),
        (obs_hbm, obs_ref),
        (var_hbm, var_ref),
        (ens_hbm.at[group], ensemble_in.at[mem]),
    ):
        fetches.append(pltpu.make_async_copy(src, dst, loads.at[len(fetches)]))
    for fetch in fetches:
        fetch.start()

    barrier = pltpu.get_barrier_semaphore()
    greeted = (
        [mem_peer(j) for j in range(1, NM)]
        + [y_at(j) for j in range(1, NY)]
        + [z_at(j) for j in range(1, NZ)]
    )
    for device in greeted:
        pl.semaphore_signal(barrier, inc=1, device_id=device, device_id_type=MESH)

    eye = (
        lax.broadcasted_iota(jnp.int32, (CM, CM), 0) == lax.broadcasted_iota(jnp.int32, (CM, CM), 1)
    )
    turn = jnp.concatenate(
        [jnp.where(eye, 1.0, 0.0), jnp.ones((16, CM), jnp.float32)], axis=0
    ).astype(jnp.bfloat16)
    for i in range(NS // KT):
        at = pl.ds(i * KT, KT)
        fetches[i].wait()
        turned = lax.dot_general(turn, m_ref[at, :], NT, preferred_element_type=jnp.float32)
        raw[:, at] = turned[:CM].astype(jnp.bfloat16)
        sums[mem, :, at] = turned[CM : CM + 1]
    for fetch in fetches[NS // KT :]:
        fetch.wait()

    pl.semaphore_wait(barrier, len(greeted))

    own = pl.ds(pl.multiple_of(k * CM, CM), CM)
    other = pl.ds(pl.multiple_of((1 - k) * CM, CM), CM)
    first_seven = pl.ds(0, NM - 1)

    def to_mem(here, landing):
        return start([(here, here, mem_peer(j)) for j in range(1, NM)], landing)

    sum_copies = to_mem(sums.at[mem], sums.at[first_seven])
    near_copies = []
    for first, count in zip(STARTS, CHUNKS, strict=True):
        rows = pl.ds(first, count)
        if first + count < CM:
            near_copies.append([start([(raw.at[rows], near.at[rows], x_at(-1))], raw.at[rows])])
            continue
        halves = []
        for turn_of in range(2):
            lanes = pl.ds(pl.multiple_of((((c + 3) % NX) // 2 + turn_of) % 2 * HALF, HALF), HALF)
            src, dst = raw.at[rows, lanes], near.at[rows, lanes]
            halves.append(start([(src, dst, x_at(-1))], dst))
        near_copies.append(halves)
    next_half = pl.multiple_of((((c + 1) % NX) // 2) * HALF, HALF)
    prev_rows = [
        pl.ds(pl.multiple_of(k * CM + i * (CM // PREV), CM // PREV), CM // PREV) for i in range(PREV)
    ]
    prev_copies = []
    for i, to_rows in enumerate(prev_rows):
        src = raw.at[pl.ds(i * (CM // PREV), CM // PREV), pl.ds(next_half, HALF)]
        prev_copies.append(start([(src, prev.at[to_rows], x_at(1))], prev.at[to_rows]))
    shared_copies = []
    sib_copy = start([(raw, sib, sibling)], raw)
    ens_copies = to_mem(ensemble_in.at[mem], ensemble_in.at[first_seven])

    classes = cls_ref[...]
    variance = jnp.zeros((1, NS), jnp.float32)
    for level in range(8):
        variance = jnp.where(classes == level, var_ref[level], variance)
    weight = lax.rsqrt(variance)
    scale[...] = weight / math.sqrt(MEMBERS - 1)

    arrive(sum_copies)
    total = sums[0]
    for j in range(1, NM):
        total = total + sums[j]
    average = total / MEMBERS
    bases[...] = average
    innovation = weight * (obs_ref[...] - average)

    def whiten(block, at):
        return ((block.astype(jnp.float32) - bases[:, at]) * scale[:, at]).astype(jnp.bfloat16)

    for i in range(NS // KT):
        at = pl.ds(i * KT, KT)
        white[own, at] = whiten(raw[:, at], at)
    arrive(sib_copy)

    @pl.loop(0, NS // KT)
    def _(i):
        at = pl.ds(pl.multiple_of(i * KT, KT), KT)
        white[other, at] = whiten(sib[:, at], at)

    def reduce_y(q, _):
        gram_part(q)
        quarter = ROWS[q] // 4
        group = []
        for j in range(1, NY):
            target = (y + j) % NY
            rows = pl.ds(pl.multiple_of(target * quarter, 8), quarter)
            group.append((part[q].at[rows], from_y[q].at[j - 1], y_at(j)))
        return start(group, from_y[q])

    def reduce_z(q, copies):
        quarter = ROWS[q] // 4
        arrive(copies)
        mine = pl.ds(pl.multiple_of(y * quarter, 8), quarter)
        sum_y[q][...] = part[q][mine, :] + from_y[q][0] + from_y[q][1] + from_y[q][2]
        group = []
        for j in FAR_Z:
            rows, lanes = piece(ROWS[q], (z + j) % NZ)
            group.append((sum_y[q].at[rows, lanes], from_z[q].at[j - 1], z_at(j)))
        return start(group, from_z[q])

    def spread_z(q, copies):
        arrive(copies)
        rows, lanes = piece(ROWS[q], z)
        total = sum_y[q][rows, lanes]
        for j in range(NZ - 1):
            total = total + from_z[q][j]
        gather_z[q][rows, lanes] = total
        here = gather_z[q].at[rows, lanes]
        return start([(here, here, z_at(j)) for j in FAR_Z], from_z[q])

    def spread_y(q, copies):
        quarter = ROWS[q] // 4
        arrive(copies)
        blocks, first_row, count, _ = PARTS[q]
        if len(blocks) == 1:
            first = blocks[0] * CM + first_row + y * quarter
        else:
            first = (blocks[0] + y // 2) * CM + first_row + (y % 2) * quarter
        rows = pl.ds(pl.multiple_of(first, 8), quarter)
        strip[rows, :] = gather_z[q][...]
        return start([(gather_z[q], strip.at[rows], y_at(j)) for j in range(1, NY)], from_y[q])

    def finish(q, copies):
        arrive(copies)
        blocks, first_row, count, _ = PARTS[q]
        for block in blocks:
            at = pl.ds(block * CM + first_row, count)
            for i, term in enumerate(split_in_three(strip[at, :])):
                terms[i, at, :] = term

    half = pl.multiple_of((c // 2) * HALF, HALF)

    other_half = pl.multiple_of((1 - c // 2) * HALF, HALF)
    here_now = [0]

    def times_gram(left, right):
        return lax.dot_general(left, right, NT, preferred_element_type=jnp.float32)

    def gram_part(q):
        blocks, first, count, needed = PARTS[q]
        while here_now[0] < needed:
            arrive(near_copies[here_now[0]][0])
            here_now[0] += 1
        if blocks == (0,):
            rows = pl.ds(pl.multiple_of(k * CM + first, 128), count)
            part[q][...] = sum(
                times_gram(white[rows, at], white[:, at]) for at in (pl.ds(0, HALF), pl.ds(HALF, HALF))
            )
            return
        rows = pl.ds(first, count)
        at = pl.ds(half, HALF)
        left = whiten(near[rows, at], at)
        if 2 in blocks:
            part[q][pl.ds((len(blocks) - 1) * count, count)] = times_gram(left, white_prev[...])
        if 1 in blocks:
            total = times_gram(left, white[:, at])
            for copies in near_copies[needed - 1][1:]:
                arrive(copies)
            at = pl.ds(other_half, HALF)
            part[q][:count] = total + times_gram(whiten(near[rows, at], at), white[:, at])

    def small_sums(_):
        shadow = lax.dot_general(
            stacked(innovation, 16), white[own, :], NT, preferred_element_type=jnp.float32
        )
        mine = pl.ds(pl.multiple_of(k * CM, CM), CM)
        square = jnp.concatenate([part[0][:, mine], part[1][:, mine]], axis=0)
        diagonal = jnp.sum(jnp.where(eye, square, 0.0), axis=0, keepdims=True)
        small[...] = jnp.concatenate(
            [jnp.sum(shadow[:8], axis=0, keepdims=True), diagonal, jnp.zeros((6, CM), jnp.float32)],
            axis=0,
        )
        return start([(small, small_y.at[j - 1], y_at(j)) for j in range(1, NY)], small_y)

    def small_sum_y(copies):
        arrive(copies)
        small_z[NZ - 1] = small[...] + small_y[0] + small_y[1] + small_y[2]
        return start(
            [(small_z.at[NZ - 1], small_z.at[j - 1], z_at(j)) for j in FAR_Z], small_z.at[first_seven]
        )

    def small_sum_z(copies):
        arrive(copies)
        total = small_z[0]
        for j in range(1, NZ):
            total = total + small_z[j]
        small_m[mem] = total
        return to_mem(small_m.at[mem], small_m.at[first_seven])

    def first_vectors(copies):
        arrive(ens_copies)
        arrive(copies)
        center = ensemble_in[0].sum(axis=1, keepdims=True)
        for j in range(1, NM):
            center = center + ensemble_in[j].sum(axis=1, keepdims=True)
        center = center / MEMBERS
        place = lax.broadcasted_iota(jnp.int32, (8, 1), 0)
        trace = small_m[0, 1:2, :]
        for j in range(1, NM):
            trace = trace + small_m[j, 1:2, :]
        norm = (MEMBERS + jnp.sum(trace, axis=1, keepdims=True)) / MEMBERS
        norms[...] = jnp.broadcast_to(norm, (8, 128))

        def own_rows(block):
            return [
                jnp.sum(jnp.where(place == 2 * y + i, block, 0.0), axis=0, keepdims=True)
                for i in range(2)
            ]

        centers[:2, :] = jnp.concatenate(own_rows(jnp.broadcast_to(center, (8, 128))), axis=0)
        for j in range(NM):
            vec[j] = jnp.concatenate(
                own_rows(ensemble_in[j] - center)
                + [small_m[j, 0:1, :], jnp.zeros((VR - 3, CM), jnp.float32)],
                axis=0,
            )

    def share_prev(i):
        arrive(prev_copies[i])
        rows = prev.at[prev_rows[i]]
        if i == 0:
            shared_copies.append(start([(rows, rows, sibling)], prev.at[pl.ds(0, CM)]))
        else:
            start([(rows, rows, sibling)], None, shared_copies[0])

    def whiten_prev():
        arrive(shared_copies[0])

        @pl.loop(0, HALF // KT)
        def _(s):
            here = pl.ds(pl.multiple_of(s * KT, KT), KT)
            at = pl.ds(pl.multiple_of(half + s * KT, KT), KT)
            white_prev[:, here] = whiten(prev[:, here], at)

    stages = (reduce_y, reduce_z, spread_z, spread_y, finish)
    state = [None] * n
    small_state = None
    for item in ORDER:
        if item == "prev 0":
            share_prev(0)
        elif item == "prev 1":
            share_prev(1)
        elif item == "white prev":
            whiten_prev()
        elif item == "small":
            small_state = small_sums(None)
        elif item == "small y":
            small_state = small_sum_y(small_state)
        elif item == "small z":
            small_state = small_sum_z(small_state)
        elif item == "vectors":
            first_vectors(small_state)
        else:
            q, stage = item
            state[q] = stages[stage](q, state[q])

    norm = norms[:1, :1]

    def folded(rows):
        return rows[:VR] + rows[VR : 2 * VR] + rows[2 * VR : 3 * VR]

    behind = ((c + NX - 1) % NX) * 2
    ring = [x_pair(2, core) for core in range(2)]

    def times(step):
        ahead = vec[((c + 1) % NX) * 2 + k]
        down = stacked(jnp.concatenate([vec[mem], ahead], axis=1), 4 * VR)
        across = stacked(jnp.concatenate([vec[2 * c], vec[2 * c + 1]], axis=1), 4 * VR)
        back = stacked(jnp.concatenate([vec[behind], vec[behind + 1]], axis=1), 4 * VR)
        for_next = for_own = for_last = 0.0
        for i in range(3):
            for_next = for_next + times_gram(across, terms[i, CM : 2 * CM, :])
            for_next = for_next + times_gram(back, terms[i, 2 * CM :, :])
            for_last = for_last + jnp.dot(
                down[:, CM:], terms[i, 2 * CM :, :], preferred_element_type=jnp.float32
            )
        exchange[step, mem, :, :CM] = folded(for_next)
        exchange[step, mem, :, 3 * CM :] = folded(for_last)

        def same(first, count, device):
            here = exchange.at[step, mem, :, pl.ds(pl.multiple_of(first * CM, CM), count * CM)]
            return here, here, device

        def pair(first, count, chips):
            return [same(first, count, x_pair(chips, core)) for core in range(2)]

        needed = start(
            pair(0, 1, 2) + [same(3 + core, 1, device) for core, device in enumerate(ring)],
            tally.at[pl.ds(0, 22)],
        )
        for i in range(3):
            for_own = for_own + jnp.dot(
                down, terms[i, : 2 * CM, :], preferred_element_type=jnp.float32
            )
        exchange[step, mem, :, CM : 3 * CM] = folded(for_own)
        mine = pl.ds(pl.multiple_of((k + 1) * CM, CM), CM)
        exchange[step, mem, :, mine] += vec[mem]
        start(pair(0, 3, 1) + pair(1, 4, -1) + [same(1, 4, sibling)], None, needed)
        if step == 1:
            return needed, None
        late = start(
            pair(1, 2, 2)
            + [same(4 - core, 1, device) for core, device in enumerate(ring)]
            + pair(3, 2, 1)
            + pair(0, 1, -1)
            + [same(0, 1, sibling)],
            tally.at[pl.ds(0, 13)],
        )
        return needed, late

    def product(step, chip, core):
        mine = pl.ds(pl.multiple_of((core + 1) * CM, CM), CM)
        last = pl.ds(pl.multiple_of((core + 3) * CM, CM), CM)
        below, above = 2 * ((chip + NX - 1) % NX), 2 * ((chip + 1) % NX)
        at = 2 * chip
        whole = (
            exchange[step, below + core, :, pl.ds(0, CM)]
            + exchange[step, at, :, mine]
            + exchange[step, at + 1, :, mine]
            + exchange[step, above, :, last]
            + exchange[step, above + 1, :, last]
        )
        return whole / norm

    neighbours = [(c, 0), (c, 1), ((c + 1) % NX, k), ((c + NX - 1) % NX, 0), ((c + NX - 1) % NX, 1)]
    distant = [((c + 1) % NX, 1 - k), ((c + 2) % NX, 0), ((c + 2) % NX, 1)]

    def advanced(step, pieces, update):
        for chip, core in pieces:
            at = 2 * chip + core
            vec[at] = update(vec[at], product(step, chip, core))

    def one_step(old, value):
        return 1.5 * old - 0.5 * value

    needed, late = times(0)
    arrive(needed)
    advanced(0, neighbours, one_step)
    for chip, core in neighbours:
        polys[2 * chip + core] = vec[2 * chip + core]
    needed, _ = times(1)
    arrive(late)
    advanced(0, distant, one_step)
    for chip, core in distant:
        polys[2 * chip + core] = vec[2 * chip + core]
    arrive(needed)
    advanced(1, neighbours, one_step)
    needed, late = times(2)
    arrive(needed)
    advanced(2, neighbours, lambda old, value: value)
    needed, last = times(3)
    arrive(late)
    advanced(2, distant, lambda old, value: value)
    arrive(needed)
    arrive(last)
    shift = jnp.zeros((2, 1), jnp.float32)
    for chip in range(NX):
        for core in range(2):
            at = 2 * chip + core
            applied = 1.5 * polys[at] - 0.5 * (1.5 * vec[at] - 0.5 * product(3, chip, core))
            polys[at] = applied
            shift = shift + jnp.sum(applied[:2] * applied[2:3], axis=1, keepdims=True)
    shift = shift / norm / math.sqrt(MEMBERS - 1)
    rows_out[y, :2, :] = centers[:2, :1] + shift + polys[mem][:2] / jnp.sqrt(norm)
    here = rows_out.at[y]
    arrive(start([(here, here, y_at(j)) for j in range(1, NY)], rows_out.at[pl.ds(0, NY - 1)]))
    out_ref[group, :] = jnp.concatenate([rows_out[j, :2, :] for j in range(NY)], axis=0)
    here = out_ref.at[group]
    arrive(start([(here, here, z_at(j)) for j in FAR_Z], out_ref.at[pl.ds(0, 8 * (NZ - 1))]))
    drain()


def shards(modelled_reactions, observations, noise_class, class_variance, ensemble):
    f32, bf16 = jnp.float32, jnp.bfloat16
    hbm = pl.BlockSpec(memory_space=pltpu.HBM)
    scratch = [
        pltpu.VMEM((NS, CM), bf16),
        pltpu.VMEM((1, NS), f32),
        pltpu.VMEM((1, NS), jnp.int32),
        pltpu.SMEM((8,), f32),
        pltpu.VMEM((CM, NS), bf16),
        pltpu.VMEM((CM, NS), bf16),
        pltpu.VMEM((2 * CM, HALF), bf16),
        pltpu.VMEM((CM, NS), bf16),
        pltpu.VMEM((2 * CM, NS), bf16),
        pltpu.VMEM((2 * CM, HALF), bf16),
        pltpu.VMEM((NM, 1, NS), f32),
        pltpu.VMEM((1, NS), f32),
        pltpu.VMEM((1, NS), f32),
        pltpu.VMEM((NM, 8, CM), f32),
        pltpu.VMEM((8, 128), f32),
        pltpu.VMEM((8, CM), f32),
        pltpu.VMEM((NY - 1, 8, CM), f32),
        pltpu.VMEM((NZ, 8, CM), f32),
        pltpu.VMEM((NM, 8, CM), f32),
        pltpu.VMEM((3 * CM, 512), f32),
        pltpu.VMEM((3, 3 * CM, 512), bf16),
        pltpu.VMEM((NM, VR, CM), f32),
        pltpu.VMEM((NM, VR, CM), f32),
        pltpu.VMEM((4, NM, VR, WIDE), f32),
        pltpu.VMEM((NY, 8, CM), f32),
        pltpu.VMEM((8, 128), f32),
        pltpu.VMEM((22, VR, CM), f32),
        pltpu.SemaphoreType.DMA((N_LOADS,)),
        pltpu.SemaphoreType.DMA((2, N_SEMS)),
    ]
    scratch += [pltpu.VMEM((r, 512), f32) for r in ROWS]
    scratch += [pltpu.VMEM((NY - 1, r // 4, 512), f32) for r in ROWS]
    scratch += [pltpu.VMEM((r // 4, 512), f32) for r in ROWS]
    scratch += [pltpu.VMEM((NZ - 1,) + piece_shape(r), f32) for r in ROWS]
    scratch += [pltpu.VMEM((r // 4, 512), f32) for r in ROWS]
    return pl.pallas_call(
        kernel,
        out_shape=jax.ShapeDtypeStruct((64, CM), f32),
        in_specs=[hbm] * 5,
        out_specs=pl.BlockSpec(memory_space=pltpu.VMEM),
        scratch_shapes=scratch,
        compiler_params=pltpu.CompilerParams(
            collective_id=0, has_side_effects=True, vmem_limit_bytes=60 * 1024 * 1024
        ),
    )(
        class_variance,
        modelled_reactions,
        observations.reshape(1, NS),
        noise_class.reshape(1, NS),
        ensemble,
    )


def solution(mesh):
    placed = (P("dp", "mem"), P("dp"), P("dp"), P(), P(None, "mem"))
    return jax.shard_map(
        shards, mesh=mesh, in_specs=placed, out_specs=P(None, "mem"), check_vma=False
    )
```

```python
import math

import jax
import jax.numpy as jnp
from jax import lax
from jax.experimental import pallas as pl
from jax.experimental.pallas import tpu as pltpu
from jax.sharding import PartitionSpec as P

MESH = pl.DeviceIdType.MESH
NX, NY, NZ, NM = 4, 4, 8, 8
MEMBERS = 2048
CM = 256
NS = 3072
HALF = NS // 2
KT = 512
CHUNKS = (64, 64, 64, 32, 32)
STARTS = tuple(sum(CHUNKS[:i]) for i in range(len(CHUNKS)))
PARTS = (
    ((0,), 0, 128, 0),
    ((0,), 128, 128, 0),
    ((1,), 0, 64, 1),
    ((1,), 64, 64, 2),
    ((2,), 0, 128, 2),
    ((1, 2), 128, 64, 3),
    ((1, 2), 192, 32, 4),
    ((1, 2), 224, 32, 5),
)
ROWS = tuple(len(blocks) * count for blocks, _, count, _ in PARTS)
ORDER = (
    (0, 0), (1, 0), "small", (2, 0), "prev 0", (2, 1), (0, 1), (1, 1), "prev 1", (3, 0), "white prev", (4, 0),
    (2, 2), "small y", (3, 1), (1, 2), (5, 0), (0, 2), (4, 1), (3, 2), "small z", (1, 3), (6, 0), (5, 1), (7, 0),
    (0, 3), (4, 2), (6, 1), (2, 3), (3, 3), (7, 1), (5, 2), (4, 3), (6, 2), (7, 2), (5, 3), (1, 4), (6, 3),
    "vectors", (7, 3), (0, 4), (4, 4), (6, 4), (5, 4), (3, 4), (2, 4), (7, 4),
)
PREV = 2
VR = 4
WIDE = 5 * CM
N_SEMS = 4 * len(ROWS) + len(CHUNKS) + 1 + PREV + 1 + 3 + 3 + 7 + 2
N_LOADS = NS // KT + 4
FAR_Z = (4, 3, 5, 2, 6, 1, 7)
NT = (((1,), (1,)), ((), ()))


def piece(rows, index):
    groups = rows // 4 // 8
    lanes = NZ // groups
    width = 512 // lanes
    return (
        pl.ds(pl.multiple_of((index // lanes) * 8, 8), 8),
        pl.ds(pl.multiple_of((index % lanes) * width, 128), width),
    )


def piece_shape(rows):
    return (8, 512 // (NZ // (rows // 4 // 8)))


def split_in_three(value):
    high = value.astype(jnp.bfloat16)
    rest = value - high.astype(jnp.float32)
    middle = rest.astype(jnp.bfloat16)
    return high, middle, (rest - middle.astype(jnp.float32)).astype(jnp.bfloat16)


def stacked(value, rows):
    terms = [term.astype(jnp.float32) for term in split_in_three(value)]
    spare = rows - 3 * value.shape[0]
    return jnp.concatenate(
        terms + [jnp.zeros((spare, value.shape[1]), jnp.float32)], axis=0
    ).astype(jnp.bfloat16)


def kernel(var_hbm, m_hbm, obs_hbm, cls_hbm, ens_hbm, out_ref, *scratch):
    (
        m_ref, obs_ref, cls_ref, var_ref, raw, near, prev, sib, white, white_prev, sums, scale, bases,
        ensemble_in, centers, small, small_y, small_z, small_m, strip, terms, vec, polys, exchange,
        rows_out, plane, norms, tally, loads, sems,
    ) = scratch[:30]
    lists = scratch[30:]
    n = len(ROWS)
    part, from_y, sum_y, from_z, gather_z = (lists[i * n : (i + 1) * n] for i in range(5))

    dp, mem = lax.axis_index("dp"), lax.axis_index("mem")
    z, y = dp // NY, dp % NY
    c, k = mem // 2, mem % 2

    def x_at(offset):
        return (dp, ((c + offset + NX) % NX) * 2 + k)

    others = [(2, 0), (2, 1), (1, 0), (-1, 0), (1, 1), (-1, 1), (0, 1)]

    def x_pair(chips, core):
        return (dp, ((c + chips + NX) % NX) * 2 + core)

    def mem_peer(j):
        chips, cores = others[j - 1]
        return x_pair(chips, (k + cores) % 2)

    def y_at(offset):
        return (z * NY + (y + offset) % NY, mem)

    def z_at(offset):
        return (((z + offset) % NZ) * NY + y, mem)

    sibling = (dp, mem + 1 - 2 * k)
    started = []

    def start(group, landing, i=None):
        if i is None:
            i = len(started)
            started.append(landing)
        for src, dst, device in group:
            pltpu.make_async_remote_copy(
                src_ref=src,
                dst_ref=dst,
                send_sem=sems.at[0, i],
                recv_sem=sems.at[1, i],
                device_id=device,
                device_id_type=MESH,
            ).start()
        return i

    def arrive(i):
        pltpu.make_async_copy(started[i], started[i], sems.at[1, i]).wait()

    drained = [0]

    def drain():
        for i in range(drained[0], len(started)):
            pltpu.make_async_copy(started[i], started[i], sems.at[0, i]).wait()
        drained[0] = len(started)

    barrier = pltpu.get_barrier_semaphore()
    greeted = (
        [z_at(j) for j in FAR_Z]
        + [y_at(j) for j in (2, 1, 3)]
        + [mem_peer(j) for j in range(1, NM)]
    )
    for device in greeted:
        pl.semaphore_signal(barrier, inc=1, device_id=device, device_id_type=MESH)

    group = pl.ds(pl.multiple_of(z * 8, 8), 8)
    fetches = []
    for i in range(NS // KT):
        at = pl.ds(i * KT, KT)
        fetches.append(pltpu.make_async_copy(m_hbm.at[at], m_ref.at[at], loads.at[i]))
    for src, dst in (
        (cls_hbm, cls_ref),
        (obs_hbm, obs_ref),
        (var_hbm, var_ref),
        (ens_hbm.at[group], ensemble_in.at[mem]),
    ):
        fetches.append(pltpu.make_async_copy(src, dst, loads.at[len(fetches)]))
    for fetch in fetches:
        fetch.start()

    eye = (
        lax.broadcasted_iota(jnp.int32, (CM, CM), 0) == lax.broadcasted_iota(jnp.int32, (CM, CM), 1)
    )
    first_rows = jnp.concatenate(
        [jnp.where(eye, 1.0, 0.0)[: CHUNKS[0]], jnp.ones((16, CM), jnp.float32)], axis=0
    ).astype(jnp.bfloat16)
    other_rows = jnp.where(eye, 1.0, 0.0)[CHUNKS[0] :].astype(jnp.bfloat16)
    for i in range(NS // KT):
        at = pl.ds(i * KT, KT)
        fetches[i].wait()
        turned = lax.dot_general(first_rows, m_ref[at, :], NT, preferred_element_type=jnp.float32)
        raw[: CHUNKS[0], at] = turned[: CHUNKS[0]].astype(jnp.bfloat16)
        sums[mem, :, at] = turned[CHUNKS[0] : CHUNKS[0] + 1]
    pl.semaphore_wait(barrier, len(greeted))

    own = pl.ds(pl.multiple_of(k * CM, CM), CM)
    other = pl.ds(pl.multiple_of((1 - k) * CM, CM), CM)
    first_seven = pl.ds(0, NM - 1)

    def to_mem(here, landing):
        return start([(here, here, mem_peer(j)) for j in range(1, NM)], landing)

    sum_copies = to_mem(sums.at[mem], sums.at[first_seven])
    near_copies = []
    for first, count in zip(STARTS, CHUNKS, strict=True):
        rows = pl.ds(first, count)
        if first == CHUNKS[0]:

            @pl.loop(0, NS // KT)
            def _(i):
                at = pl.ds(pl.multiple_of(i * KT, KT), KT)
                raw[CHUNKS[0] :, at] = lax.dot_general(
                    other_rows, m_ref[at, :], NT, preferred_element_type=jnp.float32
                ).astype(jnp.bfloat16)

        if first + count < CM:
            near_copies.append([start([(raw.at[rows], near.at[rows], x_at(-1))], raw.at[rows])])
            continue
        halves = []
        for turn_of in range(2):
            lanes = pl.ds(pl.multiple_of((((c + 3) % NX) // 2 + turn_of) % 2 * HALF, HALF), HALF)
            src, dst = raw.at[rows, lanes], near.at[rows, lanes]
            halves.append(start([(src, dst, x_at(-1))], dst))
        near_copies.append(halves)
    next_half = pl.multiple_of((((c + 1) % NX) // 2) * HALF, HALF)
    prev_rows = [
        pl.ds(pl.multiple_of(k * CM + i * (CM // PREV), CM // PREV), CM // PREV) for i in range(PREV)
    ]
    prev_copies = []
    for i, to_rows in enumerate(prev_rows):
        src = raw.at[pl.ds(i * (CM // PREV), CM // PREV), pl.ds(next_half, HALF)]
        prev_copies.append(start([(src, prev.at[to_rows], x_at(1))], prev.at[to_rows]))
    shared_copies = []
    sib_copy = start([(raw, sib, sibling)], raw)
    for fetch in fetches[NS // KT :]:
        fetch.wait()
    ens_copies = to_mem(ensemble_in.at[mem], ensemble_in.at[first_seven])

    classes = cls_ref[...]
    variance = jnp.zeros((1, NS), jnp.float32)
    for level in range(8):
        variance = jnp.where(classes == level, var_ref[level], variance)
    weight = lax.rsqrt(variance)
    scale[...] = weight / math.sqrt(MEMBERS - 1)

    arrive(sum_copies)
    total = sums[0]
    for j in range(1, NM):
        total = total + sums[j]
    average = total / MEMBERS
    bases[...] = average
    innovation = weight * (obs_ref[...] - average)

    def whiten(block, at):
        return ((block.astype(jnp.float32) - bases[:, at]) * scale[:, at]).astype(jnp.bfloat16)

    for i in range(NS // KT):
        at = pl.ds(i * KT, KT)
        white[own, at] = whiten(raw[:, at], at)
    arrive(sib_copy)

    @pl.loop(0, NS // KT)
    def _(i):
        at = pl.ds(pl.multiple_of(i * KT, KT), KT)
        white[other, at] = whiten(sib[:, at], at)

    def reduce_y(q, _):
        gram_part(q)
        quarter = ROWS[q] // 4
        group = []
        for j in range(1, NY):
            target = (y + j) % NY
            rows = pl.ds(pl.multiple_of(target * quarter, 8), quarter)
            group.append((part[q].at[rows], from_y[q].at[j - 1], y_at(j)))
        return start(group, from_y[q])

    def reduce_z(q, copies):
        quarter = ROWS[q] // 4
        arrive(copies)
        mine = pl.ds(pl.multiple_of(y * quarter, 8), quarter)
        sum_y[q][...] = part[q][mine, :] + from_y[q][0] + from_y[q][1] + from_y[q][2]
        group = []
        for j in FAR_Z:
            rows, lanes = piece(ROWS[q], (z + j) % NZ)
            group.append((sum_y[q].at[rows, lanes], from_z[q].at[j - 1], z_at(j)))
        return start(group, from_z[q])

    def spread_z(q, copies):
        arrive(copies)
        rows, lanes = piece(ROWS[q], z)
        total = sum_y[q][rows, lanes]
        for j in range(NZ - 1):
            total = total + from_z[q][j]
        gather_z[q][rows, lanes] = total
        here = gather_z[q].at[rows, lanes]
        return start([(here, here, z_at(j)) for j in FAR_Z], from_z[q])

    def spread_y(q, copies):
        quarter = ROWS[q] // 4
        arrive(copies)
        blocks, first_row, count, _ = PARTS[q]
        if len(blocks) == 1:
            first = blocks[0] * CM + first_row + y * quarter
        else:
            first = (blocks[0] + y // 2) * CM + first_row + (y % 2) * quarter
        rows = pl.ds(pl.multiple_of(first, 8), quarter)
        strip[rows, :] = gather_z[q][...]
        return start([(gather_z[q], strip.at[rows], y_at(j)) for j in range(1, NY)], from_y[q])

    def finish(q, copies):
        arrive(copies)
        blocks, first_row, count, _ = PARTS[q]
        for block in blocks:
            at = pl.ds(block * CM + first_row, count)
            for i, term in enumerate(split_in_three(strip[at, :])):
                terms[i, at, :] = term

    half = pl.multiple_of((c // 2) * HALF, HALF)

    other_half = pl.multiple_of((1 - c // 2) * HALF, HALF)
    here_now = [0]

    def times_gram(left, right):
        return lax.dot_general(left, right, NT, preferred_element_type=jnp.float32)

    def gram_part(q):
        blocks, first, count, needed = PARTS[q]
        while here_now[0] < needed:
            arrive(near_copies[here_now[0]][0])
            here_now[0] += 1
        if blocks == (0,):
            rows = pl.ds(pl.multiple_of(k * CM + first, 128), count)
            part[q][...] = sum(
                times_gram(white[rows, at], white[:, at]) for at in (pl.ds(0, HALF), pl.ds(HALF, HALF))
            )
            return
        rows = pl.ds(first, count)
        at = pl.ds(half, HALF)
        left = whiten(near[rows, at], at)
        if 2 in blocks:
            part[q][pl.ds((len(blocks) - 1) * count, count)] = times_gram(left, white_prev[...])
        if 1 in blocks:
            total = times_gram(left, white[:, at])
            for copies in near_copies[needed - 1][1:]:
                arrive(copies)
            at = pl.ds(other_half, HALF)
            part[q][:count] = total + times_gram(whiten(near[rows, at], at), white[:, at])

    def small_sums(_):
        shadow = lax.dot_general(
            stacked(innovation, 16), white[own, :], NT, preferred_element_type=jnp.float32
        )
        mine = pl.ds(pl.multiple_of(k * CM, CM), CM)
        square = jnp.concatenate([part[0][:, mine], part[1][:, mine]], axis=0)
        diagonal = jnp.sum(jnp.where(eye, square, 0.0), axis=0, keepdims=True)
        small[...] = jnp.concatenate(
            [jnp.sum(shadow[:8], axis=0, keepdims=True), diagonal, jnp.zeros((6, CM), jnp.float32)],
            axis=0,
        )
        return start([(small, small_y.at[j - 1], y_at(j)) for j in range(1, NY)], small_y)

    def small_sum_y(copies):
        arrive(copies)
        small_z[NZ - 1] = small[...] + small_y[0] + small_y[1] + small_y[2]
        return start(
            [(small_z.at[NZ - 1], small_z.at[j - 1], z_at(j)) for j in FAR_Z], small_z.at[first_seven]
        )

    def small_sum_z(copies):
        arrive(copies)
        total = small_z[0]
        for j in range(1, NZ):
            total = total + small_z[j]
        small_m[mem] = total
        return to_mem(small_m.at[mem], small_m.at[first_seven])

    def first_vectors(copies):
        arrive(ens_copies)
        arrive(copies)
        center = ensemble_in[0].sum(axis=1, keepdims=True)
        for j in range(1, NM):
            center = center + ensemble_in[j].sum(axis=1, keepdims=True)
        center = center / MEMBERS
        place = lax.broadcasted_iota(jnp.int32, (8, 1), 0)
        trace = small_m[0, 1:2, :]
        for j in range(1, NM):
            trace = trace + small_m[j, 1:2, :]
        norm = (MEMBERS + jnp.sum(trace, axis=1, keepdims=True)) / MEMBERS
        norms[...] = jnp.broadcast_to(norm, (8, 128))

        def own_rows(block):
            return [
                jnp.sum(jnp.where(place == 2 * y + i, block, 0.0), axis=0, keepdims=True)
                for i in range(2)
            ]

        centers[:2, :] = jnp.concatenate(own_rows(jnp.broadcast_to(center, (8, 128))), axis=0)
        for j in range(NM):
            vec[j] = jnp.concatenate(
                own_rows(ensemble_in[j] - center)
                + [small_m[j, 0:1, :], jnp.zeros((VR - 3, CM), jnp.float32)],
                axis=0,
            )

    def share_prev(i):
        arrive(prev_copies[i])
        rows = prev.at[prev_rows[i]]
        if i == 0:
            shared_copies.append(start([(rows, rows, sibling)], prev.at[pl.ds(0, CM)]))
        else:
            start([(rows, rows, sibling)], None, shared_copies[0])

    def whiten_prev():
        arrive(shared_copies[0])

        @pl.loop(0, HALF // KT)
        def _(s):
            here = pl.ds(pl.multiple_of(s * KT, KT), KT)
            at = pl.ds(pl.multiple_of(half + s * KT, KT), KT)
            white_prev[:, here] = whiten(prev[:, here], at)

    stages = (reduce_y, reduce_z, spread_z, spread_y, finish)
    state = [None] * n
    small_state = None
    for item in ORDER:
        if item == "prev 0":
            share_prev(0)
        elif item == "prev 1":
            share_prev(1)
        elif item == "white prev":
            whiten_prev()
        elif item == "small":
            small_state = small_sums(None)
        elif item == "small y":
            small_state = small_sum_y(small_state)
        elif item == "small z":
            small_state = small_sum_z(small_state)
        elif item == "vectors":
            first_vectors(small_state)
        else:
            q, stage = item
            state[q] = stages[stage](q, state[q])

    norm = norms[:1, :1]

    def folded(rows):
        return rows[:VR] + rows[VR : 2 * VR] + rows[2 * VR : 3 * VR]

    behind = ((c + NX - 1) % NX) * 2
    ring = [x_pair(2, core) for core in range(2)]

    def times(step):
        ahead = vec[((c + 1) % NX) * 2 + k]
        down = stacked(jnp.concatenate([vec[mem], ahead], axis=1), 4 * VR)
        across = stacked(jnp.concatenate([vec[2 * c], vec[2 * c + 1]], axis=1), 4 * VR)
        back = stacked(jnp.concatenate([vec[behind], vec[behind + 1]], axis=1), 4 * VR)
        for_next = for_own = for_last = 0.0
        for i in range(3):
            for_next = for_next + times_gram(across, terms[i, CM : 2 * CM, :])
            for_next = for_next + times_gram(back, terms[i, 2 * CM :, :])
            for_last = for_last + jnp.dot(
                down[:, CM:], terms[i, 2 * CM :, :], preferred_element_type=jnp.float32
            )
        exchange[step, mem, :, :CM] = folded(for_next)
        exchange[step, mem, :, 3 * CM :] = folded(for_last)

        def same(first, count, device):
            here = exchange.at[step, mem, :, pl.ds(pl.multiple_of(first * CM, CM), count * CM)]
            return here, here, device

        def pair(first, count, chips):
            return [same(first, count, x_pair(chips, core)) for core in range(2)]

        needed = start(
            pair(0, 1, 2) + [same(3 + core, 1, device) for core, device in enumerate(ring)],
            tally.at[pl.ds(0, 22)],
        )
        for i in range(3):
            for_own = for_own + jnp.dot(
                down, terms[i, : 2 * CM, :], preferred_element_type=jnp.float32
            )
        exchange[step, mem, :, CM : 3 * CM] = folded(for_own)
        mine = pl.ds(pl.multiple_of((k + 1) * CM, CM), CM)
        exchange[step, mem, :, mine] += vec[mem]
        start(pair(0, 3, 1) + pair(1, 4, -1) + [same(1, 4, sibling)], None, needed)
        if step == 1:
            return needed, None
        late = start(
            pair(1, 2, 2)
            + [same(4 - core, 1, device) for core, device in enumerate(ring)]
            + pair(3, 2, 1)
            + pair(0, 1, -1)
            + [same(0, 1, sibling)],
            tally.at[pl.ds(0, 13)],
        )
        return needed, late

    def product(step, chip, core):
        mine = pl.ds(pl.multiple_of((core + 1) * CM, CM), CM)
        last = pl.ds(pl.multiple_of((core + 3) * CM, CM), CM)
        below, above = 2 * ((chip + NX - 1) % NX), 2 * ((chip + 1) % NX)
        at = 2 * chip
        whole = (
            exchange[step, below + core, :, pl.ds(0, CM)]
            + exchange[step, at, :, mine]
            + exchange[step, at + 1, :, mine]
            + exchange[step, above, :, last]
            + exchange[step, above + 1, :, last]
        )
        return whole / norm

    neighbours = [(c, 0), (c, 1), ((c + 1) % NX, k), ((c + NX - 1) % NX, 0), ((c + NX - 1) % NX, 1)]
    distant = [((c + 1) % NX, 1 - k), ((c + 2) % NX, 0), ((c + 2) % NX, 1)]

    def advanced(step, pieces, update):
        for chip, core in pieces:
            at = 2 * chip + core
            vec[at] = update(vec[at], product(step, chip, core))

    def one_step(old, value):
        return 1.5 * old - 0.5 * value

    needed, late = times(0)
    arrive(needed)
    advanced(0, neighbours, one_step)
    for chip, core in neighbours:
        polys[2 * chip + core] = vec[2 * chip + core]
    before = len(started)
    needed, _ = times(1)
    for i in range(before):
        pltpu.make_async_copy(started[i], started[i], sems.at[0, i]).wait()
    drained[0] = before
    arrive(late)
    advanced(0, distant, one_step)
    for chip, core in distant:
        polys[2 * chip + core] = vec[2 * chip + core]
    arrive(needed)
    advanced(1, neighbours, one_step)
    needed, late = times(2)
    arrive(needed)
    advanced(2, neighbours, lambda old, value: value)
    needed, last = times(3)
    arrive(late)
    advanced(2, distant, lambda old, value: value)
    arrive(needed)
    arrive(last)
    shift = jnp.zeros((2, 1), jnp.float32)
    for chip in range(NX):
        for core in range(2):
            at = 2 * chip + core
            applied = 1.5 * polys[at] - 0.5 * (1.5 * vec[at] - 0.5 * product(3, chip, core))
            polys[at] = applied
            shift = shift + jnp.sum(applied[:2] * applied[2:3], axis=1, keepdims=True)
    shift = shift / norm / math.sqrt(MEMBERS - 1)
    rows_out[y, :2, :] = centers[:2, :1] + shift + polys[mem][:2] / jnp.sqrt(norm)
    here = rows_out.at[y]
    arrive(start([(here, here, y_at(j)) for j in range(1, NY)], rows_out.at[pl.ds(0, NY - 1)]))
    plane[...] = jnp.concatenate([rows_out[j, :2, :] for j in range(NY)], axis=0)
    here = out_ref.at[group]
    planes = start([(plane, here, z_at(j)) for j in FAR_Z], out_ref.at[pl.ds(0, 8 * (NZ - 1))])
    stored = pltpu.make_async_copy(plane, here, loads.at[0])
    stored.start()
    arrive(planes)
    stored.wait()
    drain()


def shards(modelled_reactions, observations, noise_class, class_variance, ensemble):
    f32, bf16 = jnp.float32, jnp.bfloat16
    hbm = pl.BlockSpec(memory_space=pltpu.HBM)
    scratch = [
        pltpu.VMEM((NS, CM), bf16),
        pltpu.VMEM((1, NS), f32),
        pltpu.VMEM((1, NS), jnp.int32),
        pltpu.SMEM((8,), f32),
        pltpu.VMEM((CM, NS), bf16),
        pltpu.VMEM((CM, NS), bf16),
        pltpu.VMEM((2 * CM, HALF), bf16),
        pltpu.VMEM((CM, NS), bf16),
        pltpu.VMEM((2 * CM, NS), bf16),
        pltpu.VMEM((2 * CM, HALF), bf16),
        pltpu.VMEM((NM, 1, NS), f32),
        pltpu.VMEM((1, NS), f32),
        pltpu.VMEM((1, NS), f32),
        pltpu.VMEM((NM, 8, CM), f32),
        pltpu.VMEM((8, 128), f32),
        pltpu.VMEM((8, CM), f32),
        pltpu.VMEM((NY - 1, 8, CM), f32),
        pltpu.VMEM((NZ, 8, CM), f32),
        pltpu.VMEM((NM, 8, CM), f32),
        pltpu.VMEM((3 * CM, 512), f32),
        pltpu.VMEM((3, 3 * CM, 512), bf16),
        pltpu.VMEM((NM, VR, CM), f32),
        pltpu.VMEM((NM, VR, CM), f32),
        pltpu.VMEM((4, NM, VR, WIDE), f32),
        pltpu.VMEM((NY, 8, CM), f32),
        pltpu.VMEM((8, CM), f32),
        pltpu.VMEM((8, 128), f32),
        pltpu.VMEM((22, VR, CM), f32),
        pltpu.SemaphoreType.DMA((N_LOADS,)),
        pltpu.SemaphoreType.DMA((2, N_SEMS)),
    ]
    scratch += [pltpu.VMEM((r, 512), f32) for r in ROWS]
    scratch += [pltpu.VMEM((NY - 1, r // 4, 512), f32) for r in ROWS]
    scratch += [pltpu.VMEM((r // 4, 512), f32) for r in ROWS]
    scratch += [pltpu.VMEM((NZ - 1,) + piece_shape(r), f32) for r in ROWS]
    scratch += [pltpu.VMEM((r // 4, 512), f32) for r in ROWS]
    return pl.pallas_call(
        kernel,
        out_shape=jax.ShapeDtypeStruct((64, CM), f32),
        in_specs=[hbm] * 5,
        out_specs=hbm,
        scratch_shapes=scratch,
        compiler_params=pltpu.CompilerParams(
            collective_id=0, has_side_effects=True, vmem_limit_bytes=60 * 1024 * 1024
        ),
    )(
        class_variance,
        modelled_reactions,
        observations.reshape(1, NS),
        noise_class.reshape(1, NS),
        ensemble,
    )


def solution(mesh):
    placed = (P("dp", "mem"), P("dp"), P("dp"), P(), P(None, "mem"))
    return jax.shard_map(
        shards, mesh=mesh, in_specs=placed, out_specs=P(None, "mem"), check_vma=False
    )
```

```python
import math

import jax
import jax.numpy as jnp
from jax import lax
from jax.experimental import pallas as pl
from jax.experimental.pallas import tpu as pltpu
from jax.sharding import PartitionSpec as P

MESH = pl.DeviceIdType.MESH
NX, NY, NZ, NM = 4, 4, 8, 8
MEMBERS = 2048
CM = 256
NS = 3072
HALF = NS // 2
KT = 512
CHUNKS = (64, 64, 32, 32, 32, 16, 16)
STARTS = tuple(sum(CHUNKS[:i]) for i in range(len(CHUNKS)))
PARTS = (
    ((0,), 0, 128, 0),
    ((0,), 128, 128, 0),
    ((1,), 0, 64, 1),
    ((1,), 64, 64, 2),
    ((2,), 0, 128, 2),
    ((1, 2), 128, 32, 3),
    ((1, 2), 160, 32, 4),
    ((1, 2), 192, 32, 5),
    ((1, 2), 224, 16, 6),
    ((1, 2), 240, 16, 7),
)
ROWS = tuple(len(blocks) * count for blocks, _, count, _ in PARTS)
ORDER = (
    (0, 0), (1, 0), "small", (2, 0), "small y", "prev 0", (0, 1), (1, 1), "prev 1", (3, 0), (0, 2),
    "white prev", (4, 0), (2, 1), (3, 1), (5, 0), (1, 2), "small z", (6, 0), (4, 1), (2, 2), (0, 3),
    (5, 1), (7, 0), (3, 2), (6, 1), (8, 0), (4, 2), (9, 0), (5, 2), (7, 1), (1, 3), (8, 1), (3, 3), (0, 4),
    (6, 2), (9, 1), (5, 3), (4, 3), (7, 2), (8, 2), (2, 3), (6, 3), (9, 2), (7, 3), "vectors", (5, 4),
    (3, 4), (6, 4), (1, 4), (4, 4), (8, 3), (2, 4), (9, 3), (7, 4),
)
SHORT = 32
PREV = 2
VR = 4
WIDE = 5 * CM
N_SEMS = 4 * len(ROWS) + len(CHUNKS) + 1 + PREV + 1 + 3 + 3 + 7 + 2
N_LOADS = NS // KT + 4
FAR_Z = (4, 3, 5, 2, 6, 1, 7)
NT = (((1,), (1,)), ((), ()))


def piece(rows, index):
    groups = rows // 4 // 8
    lanes = NZ // groups
    width = 512 // lanes
    return (
        pl.ds(pl.multiple_of((index // lanes) * 8, 8), 8),
        pl.ds(pl.multiple_of((index % lanes) * width, 128), width),
    )


def piece_shape(rows):
    if rows == SHORT:
        return (rows // 4, 512)
    return (8, 512 // (NZ // (rows // 4 // 8)))


def split_in_three(value):
    high = value.astype(jnp.bfloat16)
    rest = value - high.astype(jnp.float32)
    middle = rest.astype(jnp.bfloat16)
    return high, middle, (rest - middle.astype(jnp.float32)).astype(jnp.bfloat16)


def stacked(value, rows):
    terms = [term.astype(jnp.float32) for term in split_in_three(value)]
    spare = rows - 3 * value.shape[0]
    return jnp.concatenate(
        terms + [jnp.zeros((spare, value.shape[1]), jnp.float32)], axis=0
    ).astype(jnp.bfloat16)


def kernel(var_hbm, m_hbm, obs_hbm, cls_hbm, ens_hbm, out_ref, *scratch):
    (
        m_ref, obs_ref, cls_ref, var_ref, raw, near, prev, sib, white, white_prev, sums, scale, bases,
        ensemble_in, centers, small, small_y, small_z, small_m, strip, terms, vec, polys, exchange,
        rows_out, plane, norms, tally, loads, sems,
    ) = scratch[:30]
    lists = scratch[30:]
    n = len(ROWS)
    part, from_y, sum_y, from_z, gather_z = (lists[i * n : (i + 1) * n] for i in range(5))

    dp, mem = lax.axis_index("dp"), lax.axis_index("mem")
    z, y = dp // NY, dp % NY
    c, k = mem // 2, mem % 2

    def x_at(offset):
        return (dp, ((c + offset + NX) % NX) * 2 + k)

    others = [(2, 0), (2, 1), (1, 0), (-1, 0), (1, 1), (-1, 1), (0, 1)]

    def x_pair(chips, core):
        return (dp, ((c + chips + NX) % NX) * 2 + core)

    def mem_peer(j):
        chips, cores = others[j - 1]
        return x_pair(chips, (k + cores) % 2)

    def y_at(offset):
        return (z * NY + (y + offset) % NY, mem)

    def z_at(offset):
        return (((z + offset) % NZ) * NY + y, mem)

    sibling = (dp, mem + 1 - 2 * k)
    started = []

    def start(group, landing, i=None):
        if i is None:
            i = len(started)
            started.append(landing)
        for src, dst, device in group:
            pltpu.make_async_remote_copy(
                src_ref=src,
                dst_ref=dst,
                send_sem=sems.at[0, i],
                recv_sem=sems.at[1, i],
                device_id=device,
                device_id_type=MESH,
            ).start()
        return i

    def arrive(i):
        pltpu.make_async_copy(started[i], started[i], sems.at[1, i]).wait()

    drained = [0]

    def drain():
        for i in range(drained[0], len(started)):
            pltpu.make_async_copy(started[i], started[i], sems.at[0, i]).wait()
        drained[0] = len(started)

    barrier = pltpu.get_barrier_semaphore()
    greeted = (
        [z_at(j) for j in FAR_Z]
        + [y_at(j) for j in (2, 1, 3)]
        + [mem_peer(j) for j in range(1, NM)]
    )
    for device in greeted:
        pl.semaphore_signal(barrier, inc=1, device_id=device, device_id_type=MESH)

    group = pl.ds(pl.multiple_of(z * 8, 8), 8)
    fetches = []
    for i in range(NS // KT):
        at = pl.ds(i * KT, KT)
        fetches.append(pltpu.make_async_copy(m_hbm.at[at], m_ref.at[at], loads.at[i]))
    for src, dst in (
        (cls_hbm, cls_ref),
        (obs_hbm, obs_ref),
        (var_hbm, var_ref),
        (ens_hbm.at[group], ensemble_in.at[mem]),
    ):
        fetches.append(pltpu.make_async_copy(src, dst, loads.at[len(fetches)]))
    for fetch in fetches:
        fetch.start()

    eye = (
        lax.broadcasted_iota(jnp.int32, (CM, CM), 0) == lax.broadcasted_iota(jnp.int32, (CM, CM), 1)
    )
    first_rows = jnp.concatenate(
        [jnp.where(eye, 1.0, 0.0)[: CHUNKS[0]], jnp.ones((16, CM), jnp.float32)], axis=0
    ).astype(jnp.bfloat16)
    other_rows = jnp.where(eye, 1.0, 0.0)[CHUNKS[0] :].astype(jnp.bfloat16)
    for i in range(NS // KT):
        at = pl.ds(i * KT, KT)
        fetches[i].wait()
        turned = lax.dot_general(first_rows, m_ref[at, :], NT, preferred_element_type=jnp.float32)
        raw[: CHUNKS[0], at] = turned[: CHUNKS[0]].astype(jnp.bfloat16)
        sums[mem, :, at] = turned[CHUNKS[0] : CHUNKS[0] + 1]
    pl.semaphore_wait(barrier, len(greeted))

    own = pl.ds(pl.multiple_of(k * CM, CM), CM)
    other = pl.ds(pl.multiple_of((1 - k) * CM, CM), CM)
    first_seven = pl.ds(0, NM - 1)

    def to_mem(here, landing):
        return start([(here, here, mem_peer(j)) for j in range(1, NM)], landing)

    sum_copies = to_mem(sums.at[mem], sums.at[first_seven])
    near_copies = []
    for first, count in zip(STARTS, CHUNKS, strict=True):
        rows = pl.ds(first, count)
        if first == CHUNKS[0]:

            @pl.loop(0, NS // KT)
            def _(i):
                at = pl.ds(pl.multiple_of(i * KT, KT), KT)
                raw[CHUNKS[0] :, at] = lax.dot_general(
                    other_rows, m_ref[at, :], NT, preferred_element_type=jnp.float32
                ).astype(jnp.bfloat16)

        if first + count < CM:
            near_copies.append([start([(raw.at[rows], near.at[rows], x_at(-1))], raw.at[rows])])
            continue
        halves = []
        for turn_of in range(2):
            lanes = pl.ds(pl.multiple_of((((c + 3) % NX) // 2 + turn_of) % 2 * HALF, HALF), HALF)
            src, dst = raw.at[rows, lanes], near.at[rows, lanes]
            halves.append(start([(src, dst, x_at(-1))], dst))
        near_copies.append(halves)
    next_half = pl.multiple_of((((c + 1) % NX) // 2) * HALF, HALF)
    prev_rows = [
        pl.ds(pl.multiple_of(k * CM + i * (CM // PREV), CM // PREV), CM // PREV) for i in range(PREV)
    ]
    prev_copies = []
    for i, to_rows in enumerate(prev_rows):
        src = raw.at[pl.ds(i * (CM // PREV), CM // PREV), pl.ds(next_half, HALF)]
        prev_copies.append(start([(src, prev.at[to_rows], x_at(1))], prev.at[to_rows]))
    shared_copies = []
    sib_copy = start([(raw, sib, sibling)], raw)
    for fetch in fetches[NS // KT :]:
        fetch.wait()
    ens_copies = to_mem(ensemble_in.at[mem], ensemble_in.at[first_seven])

    classes = cls_ref[...]
    variance = jnp.zeros((1, NS), jnp.float32)
    for level in range(8):
        variance = jnp.where(classes == level, var_ref[level], variance)
    weight = lax.rsqrt(variance)
    scale[...] = weight / math.sqrt(MEMBERS - 1)

    arrive(sum_copies)
    total = sums[0]
    for j in range(1, NM):
        total = total + sums[j]
    average = total / MEMBERS
    bases[...] = average
    innovation = weight * (obs_ref[...] - average)

    def whiten(block, at):
        return ((block.astype(jnp.float32) - bases[:, at]) * scale[:, at]).astype(jnp.bfloat16)

    for i in range(NS // KT):
        at = pl.ds(i * KT, KT)
        white[own, at] = whiten(raw[:, at], at)
    arrive(sib_copy)

    @pl.loop(0, NS // KT)
    def _(i):
        at = pl.ds(pl.multiple_of(i * KT, KT), KT)
        white[other, at] = whiten(sib[:, at], at)

    def reduce_y(q, _):
        gram_part(q)
        quarter = ROWS[q] // 4
        group = []
        for j in range(1, NY):
            target = (y + j) % NY
            rows = pl.ds(pl.multiple_of(target * quarter, 8), quarter)
            group.append((part[q].at[rows], from_y[q].at[j - 1], y_at(j)))
        return start(group, from_y[q])

    def reduce_z(q, copies):
        quarter = ROWS[q] // 4
        arrive(copies)
        mine = pl.ds(pl.multiple_of(y * quarter, 8), quarter)
        sum_y[q][...] = part[q][mine, :] + from_y[q][0] + from_y[q][1] + from_y[q][2]
        group = []
        for j in FAR_Z:
            rows, lanes = piece(ROWS[q], (z + j) % NZ)
            group.append((sum_y[q].at[rows, lanes], from_z[q].at[j - 1], z_at(j)))
        return start(group, from_z[q])

    def exchange_z(q, copies):
        arrive(copies)
        mine = pl.ds(pl.multiple_of(y * (ROWS[q] // 4), 8), ROWS[q] // 4)
        sum_y[q][...] = part[q][mine, :] + from_y[q][0] + from_y[q][1] + from_y[q][2]
        return start([(sum_y[q], from_z[q].at[j - 1], z_at(j)) for j in FAR_Z], from_z[q])

    def spread_sum(q, copies):
        arrive(copies)
        total = sum_y[q][...]
        for j in range(NZ - 1):
            total = total + from_z[q][j]
        gather_z[q][...] = total
        return give_y(q)

    def spread_z(q, copies):
        arrive(copies)
        rows, lanes = piece(ROWS[q], z)
        total = sum_y[q][rows, lanes]
        for j in range(NZ - 1):
            total = total + from_z[q][j]
        gather_z[q][rows, lanes] = total
        here = gather_z[q].at[rows, lanes]
        return start([(here, here, z_at(j)) for j in FAR_Z], from_z[q])

    def spread_y(q, copies):
        arrive(copies)
        return give_y(q)

    def give_y(q):
        quarter = ROWS[q] // 4
        blocks, first_row, count, _ = PARTS[q]
        if len(blocks) == 1:
            first = blocks[0] * CM + first_row + y * quarter
        else:
            first = (blocks[0] + y // 2) * CM + first_row + (y % 2) * quarter
        rows = pl.ds(pl.multiple_of(first, 8), quarter)
        strip[rows, :] = gather_z[q][...]
        return start([(gather_z[q], strip.at[rows], y_at(j)) for j in range(1, NY)], from_y[q])

    def finish(q, copies):
        arrive(copies)
        blocks, first_row, count, _ = PARTS[q]
        for block in blocks:
            at = pl.ds(block * CM + first_row, count)
            for i, term in enumerate(split_in_three(strip[at, :])):
                terms[i, at, :] = term

    half = pl.multiple_of((c // 2) * HALF, HALF)

    other_half = pl.multiple_of((1 - c // 2) * HALF, HALF)
    here_now = [0]

    def times_gram(left, right):
        return lax.dot_general(left, right, NT, preferred_element_type=jnp.float32)

    def gram_part(q):
        blocks, first, count, needed = PARTS[q]
        while here_now[0] < needed:
            arrive(near_copies[here_now[0]][0])
            here_now[0] += 1
        if blocks == (0,):
            rows = pl.ds(pl.multiple_of(k * CM + first, 128), count)
            part[q][...] = sum(
                times_gram(white[rows, at], white[:, at]) for at in (pl.ds(0, HALF), pl.ds(HALF, HALF))
            )
            return
        rows = pl.ds(first, count)
        at = pl.ds(half, HALF)
        left = whiten(near[rows, at], at)
        if 2 in blocks:
            part[q][pl.ds((len(blocks) - 1) * count, count)] = times_gram(left, white_prev[...])
        if 1 in blocks:
            total = times_gram(left, white[:, at])
            for copies in near_copies[needed - 1][1:]:
                arrive(copies)
            at = pl.ds(other_half, HALF)
            part[q][:count] = total + times_gram(whiten(near[rows, at], at), white[:, at])

    def small_sums(_):
        shadow = lax.dot_general(
            stacked(innovation, 16), white[own, :], NT, preferred_element_type=jnp.float32
        )
        mine = pl.ds(pl.multiple_of(k * CM, CM), CM)
        square = jnp.concatenate([part[0][:, mine], part[1][:, mine]], axis=0)
        diagonal = jnp.sum(jnp.where(eye, square, 0.0), axis=0, keepdims=True)
        small[...] = jnp.concatenate(
            [jnp.sum(shadow[:8], axis=0, keepdims=True), diagonal, jnp.zeros((6, CM), jnp.float32)],
            axis=0,
        )
        return start([(small, small_y.at[j - 1], y_at(j)) for j in range(1, NY)], small_y)

    def small_sum_y(copies):
        arrive(copies)
        small_z[NZ - 1] = small[...] + small_y[0] + small_y[1] + small_y[2]
        return start(
            [(small_z.at[NZ - 1], small_z.at[j - 1], z_at(j)) for j in FAR_Z], small_z.at[first_seven]
        )

    def small_sum_z(copies):
        arrive(copies)
        total = small_z[0]
        for j in range(1, NZ):
            total = total + small_z[j]
        small_m[mem] = total
        return to_mem(small_m.at[mem], small_m.at[first_seven])

    def first_vectors(copies):
        arrive(ens_copies)
        arrive(copies)
        center = ensemble_in[0].sum(axis=1, keepdims=True)
        for j in range(1, NM):
            center = center + ensemble_in[j].sum(axis=1, keepdims=True)
        center = center / MEMBERS
        place = lax.broadcasted_iota(jnp.int32, (8, 1), 0)
        trace = small_m[0, 1:2, :]
        for j in range(1, NM):
            trace = trace + small_m[j, 1:2, :]
        norm = (MEMBERS + jnp.sum(trace, axis=1, keepdims=True)) / MEMBERS
        norms[...] = jnp.broadcast_to(norm, (8, 128))

        def own_rows(block):
            return [
                jnp.sum(jnp.where(place == 2 * y + i, block, 0.0), axis=0, keepdims=True)
                for i in range(2)
            ]

        centers[:2, :] = jnp.concatenate(own_rows(jnp.broadcast_to(center, (8, 128))), axis=0)
        for j in range(NM):
            vec[j] = jnp.concatenate(
                own_rows(ensemble_in[j] - center)
                + [small_m[j, 0:1, :], jnp.zeros((VR - 3, CM), jnp.float32)],
                axis=0,
            )

    def share_prev(i):
        arrive(prev_copies[i])
        rows = prev.at[prev_rows[i]]
        if i == 0:
            shared_copies.append(start([(rows, rows, sibling)], prev.at[pl.ds(0, CM)]))
        else:
            start([(rows, rows, sibling)], None, shared_copies[0])

    def whiten_prev():
        arrive(shared_copies[0])

        @pl.loop(0, HALF // KT)
        def _(s):
            here = pl.ds(pl.multiple_of(s * KT, KT), KT)
            at = pl.ds(pl.multiple_of(half + s * KT, KT), KT)
            white_prev[:, here] = whiten(prev[:, here], at)

    usual = (reduce_y, reduce_z, spread_z, spread_y, finish)
    short = (reduce_y, exchange_z, spread_sum, finish)
    state = [None] * n
    small_state = None
    for item in ORDER:
        if item == "prev 0":
            share_prev(0)
        elif item == "prev 1":
            share_prev(1)
        elif item == "white prev":
            whiten_prev()
        elif item == "small":
            small_state = small_sums(None)
        elif item == "small y":
            small_state = small_sum_y(small_state)
        elif item == "small z":
            small_state = small_sum_z(small_state)
        elif item == "vectors":
            first_vectors(small_state)
        else:
            q, stage = item
            state[q] = (short if ROWS[q] == SHORT else usual)[stage](q, state[q])

    norm = norms[:1, :1]

    def folded(rows):
        return rows[:VR] + rows[VR : 2 * VR] + rows[2 * VR : 3 * VR]

    behind = ((c + NX - 1) % NX) * 2
    ring = [x_pair(2, core) for core in range(2)]

    def times(step):
        ahead = vec[((c + 1) % NX) * 2 + k]
        down = stacked(jnp.concatenate([vec[mem], ahead], axis=1), 4 * VR)
        across = stacked(jnp.concatenate([vec[2 * c], vec[2 * c + 1]], axis=1), 4 * VR)
        back = stacked(jnp.concatenate([vec[behind], vec[behind + 1]], axis=1), 4 * VR)
        for_next = for_own = for_last = 0.0
        for i in range(3):
            for_next = for_next + times_gram(across, terms[i, CM : 2 * CM, :])
            for_next = for_next + times_gram(back, terms[i, 2 * CM :, :])
            for_last = for_last + jnp.dot(
                down[:, CM:], terms[i, 2 * CM :, :], preferred_element_type=jnp.float32
            )
        exchange[step, mem, :, :CM] = folded(for_next)
        exchange[step, mem, :, 3 * CM :] = folded(for_last)

        def same(first, count, device):
            here = exchange.at[step, mem, :, pl.ds(pl.multiple_of(first * CM, CM), count * CM)]
            return here, here, device

        def pair(first, count, chips):
            return [same(first, count, x_pair(chips, core)) for core in range(2)]

        needed = start(
            pair(0, 1, 2) + [same(3 + core, 1, device) for core, device in enumerate(ring)],
            tally.at[pl.ds(0, 22)],
        )
        for i in range(3):
            for_own = for_own + jnp.dot(
                down, terms[i, : 2 * CM, :], preferred_element_type=jnp.float32
            )
        exchange[step, mem, :, CM : 3 * CM] = folded(for_own)
        mine = pl.ds(pl.multiple_of((k + 1) * CM, CM), CM)
        exchange[step, mem, :, mine] += vec[mem]
        start(pair(0, 3, 1) + pair(1, 4, -1) + [same(1, 4, sibling)], None, needed)
        if step == 1:
            return needed, None
        late = start(
            pair(1, 2, 2)
            + [same(4 - core, 1, device) for core, device in enumerate(ring)]
            + pair(3, 2, 1)
            + pair(0, 1, -1)
            + [same(0, 1, sibling)],
            tally.at[pl.ds(0, 13)],
        )
        return needed, late

    def product(step, chip, core):
        mine = pl.ds(pl.multiple_of((core + 1) * CM, CM), CM)
        last = pl.ds(pl.multiple_of((core + 3) * CM, CM), CM)
        below, above = 2 * ((chip + NX - 1) % NX), 2 * ((chip + 1) % NX)
        at = 2 * chip
        whole = (
            exchange[step, below + core, :, pl.ds(0, CM)]
            + exchange[step, at, :, mine]
            + exchange[step, at + 1, :, mine]
            + exchange[step, above, :, last]
            + exchange[step, above + 1, :, last]
        )
        return whole / norm

    neighbours = [(c, 0), (c, 1), ((c + 1) % NX, k), ((c + NX - 1) % NX, 0), ((c + NX - 1) % NX, 1)]
    distant = [((c + 1) % NX, 1 - k), ((c + 2) % NX, 0), ((c + 2) % NX, 1)]

    def advanced(step, pieces, update):
        for chip, core in pieces:
            at = 2 * chip + core
            vec[at] = update(vec[at], product(step, chip, core))

    def one_step(old, value):
        return 1.5 * old - 0.5 * value

    needed, late = times(0)
    arrive(needed)
    advanced(0, neighbours, one_step)
    for chip, core in neighbours:
        polys[2 * chip + core] = vec[2 * chip + core]
    before = len(started)
    needed, _ = times(1)
    for i in range(before):
        pltpu.make_async_copy(started[i], started[i], sems.at[0, i]).wait()
    drained[0] = before
    arrive(late)
    advanced(0, distant, one_step)
    for chip, core in distant:
        polys[2 * chip + core] = vec[2 * chip + core]
    arrive(needed)
    advanced(1, neighbours, one_step)
    needed, late = times(2)
    arrive(needed)
    advanced(2, neighbours, lambda old, value: value)
    needed, last = times(3)
    arrive(late)
    advanced(2, distant, lambda old, value: value)
    arrive(needed)
    arrive(last)
    shift = jnp.zeros((2, 1), jnp.float32)
    for chip in range(NX):
        for core in range(2):
            at = 2 * chip + core
            applied = 1.5 * polys[at] - 0.5 * (1.5 * vec[at] - 0.5 * product(3, chip, core))
            polys[at] = applied
            shift = shift + jnp.sum(applied[:2] * applied[2:3], axis=1, keepdims=True)
    shift = shift / norm / math.sqrt(MEMBERS - 1)
    rows_out[y, :2, :] = centers[:2, :1] + shift + polys[mem][:2] / jnp.sqrt(norm)
    here = rows_out.at[y]
    arrive(start([(here, here, y_at(j)) for j in range(1, NY)], rows_out.at[pl.ds(0, NY - 1)]))
    plane[...] = jnp.concatenate([rows_out[j, :2, :] for j in range(NY)], axis=0)
    here = out_ref.at[group]
    planes = start([(plane, here, z_at(j)) for j in FAR_Z], out_ref.at[pl.ds(0, 8 * (NZ - 1))])
    stored = pltpu.make_async_copy(plane, here, loads.at[0])
    stored.start()
    arrive(planes)
    stored.wait()
    drain()


def shards(modelled_reactions, observations, noise_class, class_variance, ensemble):
    f32, bf16 = jnp.float32, jnp.bfloat16
    hbm = pl.BlockSpec(memory_space=pltpu.HBM)
    scratch = [
        pltpu.VMEM((NS, CM), bf16),
        pltpu.VMEM((1, NS), f32),
        pltpu.VMEM((1, NS), jnp.int32),
        pltpu.SMEM((8,), f32),
        pltpu.VMEM((CM, NS), bf16),
        pltpu.VMEM((CM, NS), bf16),
        pltpu.VMEM((2 * CM, HALF), bf16),
        pltpu.VMEM((CM, NS), bf16),
        pltpu.VMEM((2 * CM, NS), bf16),
        pltpu.VMEM((2 * CM, HALF), bf16),
        pltpu.VMEM((NM, 1, NS), f32),
        pltpu.VMEM((1, NS), f32),
        pltpu.VMEM((1, NS), f32),
        pltpu.VMEM((NM, 8, CM), f32),
        pltpu.VMEM((8, 128), f32),
        pltpu.VMEM((8, CM), f32),
        pltpu.VMEM((NY - 1, 8, CM), f32),
        pltpu.VMEM((NZ, 8, CM), f32),
        pltpu.VMEM((NM, 8, CM), f32),
        pltpu.VMEM((3 * CM, 512), f32),
        pltpu.VMEM((3, 3 * CM, 512), bf16),
        pltpu.VMEM((NM, VR, CM), f32),
        pltpu.VMEM((NM, VR, CM), f32),
        pltpu.VMEM((4, NM, VR, WIDE), f32),
        pltpu.VMEM((NY, 8, CM), f32),
        pltpu.VMEM((8, CM), f32),
        pltpu.VMEM((8, 128), f32),
        pltpu.VMEM((22, VR, CM), f32),
        pltpu.SemaphoreType.DMA((N_LOADS,)),
        pltpu.SemaphoreType.DMA((2, N_SEMS)),
    ]
    scratch += [pltpu.VMEM((r, 512), f32) for r in ROWS]
    scratch += [pltpu.VMEM((NY - 1, r // 4, 512), f32) for r in ROWS]
    scratch += [pltpu.VMEM((r // 4, 512), f32) for r in ROWS]
    scratch += [pltpu.VMEM((NZ - 1,) + piece_shape(r), f32) for r in ROWS]
    scratch += [pltpu.VMEM((r // 4, 512), f32) for r in ROWS]
    return pl.pallas_call(
        kernel,
        out_shape=jax.ShapeDtypeStruct((64, CM), f32),
        in_specs=[hbm] * 5,
        out_specs=hbm,
        scratch_shapes=scratch,
        compiler_params=pltpu.CompilerParams(
            collective_id=0, has_side_effects=True, vmem_limit_bytes=60 * 1024 * 1024
        ),
    )(
        class_variance,
        modelled_reactions,
        observations.reshape(1, NS),
        noise_class.reshape(1, NS),
        ensemble,
    )


def solution(mesh):
    placed = (P("dp", "mem"), P("dp"), P("dp"), P(), P(None, "mem"))
    return jax.shard_map(
        shards, mesh=mesh, in_specs=placed, out_specs=P(None, "mem"), check_vma=False
    )
```

```python
import math

import jax
import jax.numpy as jnp
from jax import lax
from jax.experimental import pallas as pl
from jax.experimental.pallas import tpu as pltpu
from jax.sharding import PartitionSpec as P

MESH = pl.DeviceIdType.MESH
NX, NY, NZ, NM = 4, 4, 8, 8
MEMBERS = 2048
CM = 256
NS = 3072
HALF = NS // 2
KT = 512
CHUNKS = (64, 64, 32, 32, 32, 16, 16)
STARTS = tuple(sum(CHUNKS[:i]) for i in range(len(CHUNKS)))
PARTS = (
    ((0,), 0, 128, 0),
    ((0,), 128, 128, 0),
    ((1,), 0, 64, 1),
    ((1,), 64, 64, 2),
    ((2,), 0, 128, 2),
    ((1, 2), 128, 32, 3),
    ((1, 2), 160, 32, 4),
    ((1, 2), 192, 32, 5),
    ((1, 2), 224, 16, 6),
    ((1, 2), 240, 16, 7),
)
ROWS = tuple(len(blocks) * count for blocks, _, count, _ in PARTS)
ORDER = (
    (0, 0), (1, 0), "small", (2, 0), "small y", "prev 0", (0, 1), (1, 1), "prev 1", (3, 0), (0, 2),
    "white prev", (4, 0), (2, 1), (5, 0), (1, 2), "small z", (3, 1), (6, 0), (4, 1), (0, 3), (2, 2),
    (5, 1), (7, 0), (3, 2), (8, 0), (6, 1), (1, 3), (4, 2), (9, 0), (5, 2), (7, 1), (8, 1), (3, 3), (0, 4),
    (6, 2), (9, 1), (5, 3), (4, 3), (7, 2), (8, 2), (2, 3), (6, 3), (9, 2), (7, 3), "vectors", (5, 4),
    (3, 4), (6, 4), (1, 4), (4, 4), (8, 3), (2, 4), (9, 3), (7, 4),
)
SHORT = 32
PREV = 2
VR = 4
WIDE = 5 * CM
N_SEMS = 4 * len(ROWS) + len(CHUNKS) + 1 + PREV + 1 + 3 + 3 + 7 + 2
OWN = 13
POOL = 16
N_LOADS = NS // KT + 4
FAR_Z = (4, 3, 5, 2, 6, 1, 7)
NT = (((1,), (1,)), ((), ()))


def piece(rows, index):
    groups = rows // 4 // 8
    lanes = NZ // groups
    width = 512 // lanes
    return (
        pl.ds(pl.multiple_of((index // lanes) * 8, 8), 8),
        pl.ds(pl.multiple_of((index % lanes) * width, 128), width),
    )


def piece_shape(rows):
    if rows == SHORT:
        return (rows // 4, 512)
    return (8, 512 // (NZ // (rows // 4 // 8)))


def split_in_three(value):
    high = value.astype(jnp.bfloat16)
    rest = value - high.astype(jnp.float32)
    middle = rest.astype(jnp.bfloat16)
    return high, middle, (rest - middle.astype(jnp.float32)).astype(jnp.bfloat16)


def stacked(value, rows):
    terms = [term.astype(jnp.float32) for term in split_in_three(value)]
    spare = rows - 3 * value.shape[0]
    return jnp.concatenate(
        terms + [jnp.zeros((spare, value.shape[1]), jnp.float32)], axis=0
    ).astype(jnp.bfloat16)


def kernel(var_hbm, m_hbm, obs_hbm, cls_hbm, ens_hbm, out_ref, *scratch):
    (
        m_ref, obs_ref, cls_ref, var_ref, raw, near, prev, sib, white, white_prev, sums, scale, bases,
        ensemble_in, centers, small, small_y, small_z, small_m, strip, terms, vec, polys, exchange,
        rows_out, plane, norms, tally, loads, sends, sems,
    ) = scratch[:31]
    lists = scratch[31:]
    n = len(ROWS)
    part, from_y, sum_y, from_z, gather_z = (lists[i * n : (i + 1) * n] for i in range(5))

    dp, mem = lax.axis_index("dp"), lax.axis_index("mem")
    z, y = dp // NY, dp % NY
    c, k = mem // 2, mem % 2

    def x_at(offset):
        return (dp, ((c + offset + NX) % NX) * 2 + k)

    others = [(2, 0), (2, 1), (1, 0), (-1, 0), (1, 1), (-1, 1), (0, 1)]

    def x_pair(chips, core):
        return (dp, ((c + chips + NX) % NX) * 2 + core)

    def mem_peer(j):
        chips, cores = others[j - 1]
        return x_pair(chips, (k + cores) % 2)

    def y_at(offset):
        return (z * NY + (y + offset) % NY, mem)

    def z_at(offset):
        return (((z + offset) % NZ) * NY + y, mem)

    sibling = (dp, mem + 1 - 2 * k)
    started = []
    leaving = {}

    def slot(i):
        return i if i < OWN else OWN + (i - OWN) % POOL

    def left(at):
        landing = started[leaving.pop(at)]
        pltpu.make_async_copy(landing, landing, sends.at[at]).wait()


    def start(group, landing, i=None):
        if i is None:
            i = len(started)
            started.append(landing)
            if slot(i) in leaving:
                left(slot(i))
            leaving[slot(i)] = i
        for src, dst, device in group:
            pltpu.make_async_remote_copy(
                src_ref=src,
                dst_ref=dst,
                send_sem=sends.at[slot(i)],
                recv_sem=sems.at[i],
                device_id=device,
                device_id_type=MESH,
            ).start()
        return i

    def arrive(i):
        pltpu.make_async_copy(started[i], started[i], sems.at[i]).wait()

    def drain(before):
        for at in [at for at, i in leaving.items() if i < before]:
            left(at)

    barrier = pltpu.get_barrier_semaphore()
    greeted = (
        [z_at(j) for j in FAR_Z]
        + [y_at(j) for j in (2, 1, 3)]
        + [mem_peer(j) for j in range(1, NM)]
    )
    for device in greeted:
        pl.semaphore_signal(barrier, inc=1, device_id=device, device_id_type=MESH)

    group = pl.ds(pl.multiple_of(z * 8, 8), 8)
    fetches = []
    for i in range(NS // KT):
        at = pl.ds(i * KT, KT)
        fetches.append(pltpu.make_async_copy(m_hbm.at[at], m_ref.at[at], loads.at[i]))
    for src, dst in (
        (cls_hbm, cls_ref),
        (obs_hbm, obs_ref),
        (var_hbm, var_ref),
        (ens_hbm.at[group], ensemble_in.at[mem]),
    ):
        fetches.append(pltpu.make_async_copy(src, dst, loads.at[len(fetches)]))
    for fetch in fetches:
        fetch.start()

    eye = (
        lax.broadcasted_iota(jnp.int32, (CM, CM), 0) == lax.broadcasted_iota(jnp.int32, (CM, CM), 1)
    )
    first_rows = jnp.concatenate(
        [jnp.where(eye, 1.0, 0.0)[: CHUNKS[0]], jnp.ones((16, CM), jnp.float32)], axis=0
    ).astype(jnp.bfloat16)
    other_rows = jnp.where(eye, 1.0, 0.0)[CHUNKS[0] :].astype(jnp.bfloat16)
    for i in range(NS // KT):
        at = pl.ds(i * KT, KT)
        fetches[i].wait()
        turned = lax.dot_general(first_rows, m_ref[at, :], NT, preferred_element_type=jnp.float32)
        raw[: CHUNKS[0], at] = turned[: CHUNKS[0]].astype(jnp.bfloat16)
        sums[mem, :, at] = turned[CHUNKS[0] : CHUNKS[0] + 1]
    pl.semaphore_wait(barrier, len(greeted))

    own = pl.ds(pl.multiple_of(k * CM, CM), CM)
    other = pl.ds(pl.multiple_of((1 - k) * CM, CM), CM)
    first_seven = pl.ds(0, NM - 1)

    def to_mem(here, landing):
        return start([(here, here, mem_peer(j)) for j in range(1, NM)], landing)

    sum_copies = to_mem(sums.at[mem], sums.at[first_seven])
    near_copies = []
    for first, count in zip(STARTS, CHUNKS, strict=True):
        rows = pl.ds(first, count)
        if first == CHUNKS[0]:

            @pl.loop(0, NS // KT)
            def _(i):
                at = pl.ds(pl.multiple_of(i * KT, KT), KT)
                raw[CHUNKS[0] :, at] = lax.dot_general(
                    other_rows, m_ref[at, :], NT, preferred_element_type=jnp.float32
                ).astype(jnp.bfloat16)

        if first + count < CM:
            near_copies.append([start([(raw.at[rows], near.at[rows], x_at(-1))], raw.at[rows])])
            continue
        halves = []
        for turn_of in range(2):
            lanes = pl.ds(pl.multiple_of((((c + 3) % NX) // 2 + turn_of) % 2 * HALF, HALF), HALF)
            src, dst = raw.at[rows, lanes], near.at[rows, lanes]
            halves.append(start([(src, dst, x_at(-1))], dst))
        near_copies.append(halves)
    next_half = pl.multiple_of((((c + 1) % NX) // 2) * HALF, HALF)
    prev_rows = [
        pl.ds(pl.multiple_of(k * CM + i * (CM // PREV), CM // PREV), CM // PREV) for i in range(PREV)
    ]
    prev_copies = []
    for i, to_rows in enumerate(prev_rows):
        src = raw.at[pl.ds(i * (CM // PREV), CM // PREV), pl.ds(next_half, HALF)]
        prev_copies.append(start([(src, prev.at[to_rows], x_at(1))], prev.at[to_rows]))
    shared_copies = []
    sib_copy = start([(raw, sib, sibling)], raw)
    for fetch in fetches[NS // KT :]:
        fetch.wait()
    ens_copies = to_mem(ensemble_in.at[mem], ensemble_in.at[first_seven])

    classes = cls_ref[...]
    variance = jnp.zeros((1, NS), jnp.float32)
    for level in range(8):
        variance = jnp.where(classes == level, var_ref[level], variance)
    weight = lax.rsqrt(variance)
    scale[...] = weight / math.sqrt(MEMBERS - 1)

    arrive(sum_copies)
    total = sums[0]
    for j in range(1, NM):
        total = total + sums[j]
    average = total / MEMBERS
    bases[...] = average
    innovation = weight * (obs_ref[...] - average)

    def whiten(block, at):
        return ((block.astype(jnp.float32) - bases[:, at]) * scale[:, at]).astype(jnp.bfloat16)

    for i in range(NS // KT):
        at = pl.ds(i * KT, KT)
        white[own, at] = whiten(raw[:, at], at)
    arrive(sib_copy)

    @pl.loop(0, NS // KT)
    def _(i):
        at = pl.ds(pl.multiple_of(i * KT, KT), KT)
        white[other, at] = whiten(sib[:, at], at)

    def reduce_y(q, _):
        gram_part(q)
        quarter = ROWS[q] // 4
        group = []
        for j in range(1, NY):
            target = (y + j) % NY
            rows = pl.ds(pl.multiple_of(target * quarter, 8), quarter)
            group.append((part[q].at[rows], from_y[q].at[j - 1], y_at(j)))
        return start(group, from_y[q])

    def reduce_z(q, copies):
        quarter = ROWS[q] // 4
        arrive(copies)
        mine = pl.ds(pl.multiple_of(y * quarter, 8), quarter)
        sum_y[q][...] = part[q][mine, :] + from_y[q][0] + from_y[q][1] + from_y[q][2]
        group = []
        for j in FAR_Z:
            rows, lanes = piece(ROWS[q], (z + j) % NZ)
            group.append((sum_y[q].at[rows, lanes], from_z[q].at[j - 1], z_at(j)))
        return start(group, from_z[q])

    def exchange_z(q, copies):
        arrive(copies)
        mine = pl.ds(pl.multiple_of(y * (ROWS[q] // 4), 8), ROWS[q] // 4)
        sum_y[q][...] = part[q][mine, :] + from_y[q][0] + from_y[q][1] + from_y[q][2]
        return start([(sum_y[q], from_z[q].at[j - 1], z_at(j)) for j in FAR_Z], from_z[q])

    def spread_sum(q, copies):
        arrive(copies)
        total = sum_y[q][...]
        for j in range(NZ - 1):
            total = total + from_z[q][j]
        gather_z[q][...] = total
        return give_y(q)

    def spread_z(q, copies):
        arrive(copies)
        rows, lanes = piece(ROWS[q], z)
        total = sum_y[q][rows, lanes]
        for j in range(NZ - 1):
            total = total + from_z[q][j]
        gather_z[q][rows, lanes] = total
        here = gather_z[q].at[rows, lanes]
        return start([(here, here, z_at(j)) for j in FAR_Z], from_z[q])

    def spread_y(q, copies):
        arrive(copies)
        return give_y(q)

    def give_y(q):
        quarter = ROWS[q] // 4
        blocks, first_row, count, _ = PARTS[q]
        if len(blocks) == 1:
            first = blocks[0] * CM + first_row + y * quarter
        else:
            first = (blocks[0] + y // 2) * CM + first_row + (y % 2) * quarter
        rows = pl.ds(pl.multiple_of(first, 8), quarter)
        strip[rows, :] = gather_z[q][...]
        return start([(gather_z[q], strip.at[rows], y_at(j)) for j in range(1, NY)], from_y[q])

    def finish(q, copies):
        arrive(copies)
        blocks, first_row, count, _ = PARTS[q]
        for block in blocks:
            at = pl.ds(block * CM + first_row, count)
            for i, term in enumerate(split_in_three(strip[at, :])):
                terms[i, at, :] = term

    half = pl.multiple_of((c // 2) * HALF, HALF)

    other_half = pl.multiple_of((1 - c // 2) * HALF, HALF)
    here_now = [0]

    def times_gram(left, right):
        return lax.dot_general(left, right, NT, preferred_element_type=jnp.float32)

    def gram_part(q):
        blocks, first, count, needed = PARTS[q]
        while here_now[0] < needed:
            arrive(near_copies[here_now[0]][0])
            here_now[0] += 1
        if blocks == (0,):
            rows = pl.ds(pl.multiple_of(k * CM + first, 128), count)
            part[q][...] = sum(
                times_gram(white[rows, at], white[:, at]) for at in (pl.ds(0, HALF), pl.ds(HALF, HALF))
            )
            return
        rows = pl.ds(first, count)
        at = pl.ds(half, HALF)
        left = whiten(near[rows, at], at)
        if 2 in blocks:
            part[q][pl.ds((len(blocks) - 1) * count, count)] = times_gram(left, white_prev[...])
        if 1 in blocks:
            total = times_gram(left, white[:, at])
            for copies in near_copies[needed - 1][1:]:
                arrive(copies)
            at = pl.ds(other_half, HALF)
            part[q][:count] = total + times_gram(whiten(near[rows, at], at), white[:, at])

    def small_sums(_):
        shadow = lax.dot_general(
            stacked(innovation, 16), white[own, :], NT, preferred_element_type=jnp.float32
        )
        mine = pl.ds(pl.multiple_of(k * CM, CM), CM)
        square = jnp.concatenate([part[0][:, mine], part[1][:, mine]], axis=0)
        diagonal = jnp.sum(jnp.where(eye, square, 0.0), axis=0, keepdims=True)
        small[...] = jnp.concatenate(
            [jnp.sum(shadow[:8], axis=0, keepdims=True), diagonal, jnp.zeros((6, CM), jnp.float32)],
            axis=0,
        )
        return start([(small, small_y.at[j - 1], y_at(j)) for j in range(1, NY)], small_y)

    def small_sum_y(copies):
        arrive(copies)
        small_z[NZ - 1] = small[...] + small_y[0] + small_y[1] + small_y[2]
        return start(
            [(small_z.at[NZ - 1], small_z.at[j - 1], z_at(j)) for j in FAR_Z], small_z.at[first_seven]
        )

    def small_sum_z(copies):
        arrive(copies)
        total = small_z[0]
        for j in range(1, NZ):
            total = total + small_z[j]
        small_m[mem] = total
        return to_mem(small_m.at[mem], small_m.at[first_seven])

    def first_vectors(copies):
        arrive(ens_copies)
        arrive(copies)
        center = ensemble_in[0].sum(axis=1, keepdims=True)
        for j in range(1, NM):
            center = center + ensemble_in[j].sum(axis=1, keepdims=True)
        center = center / MEMBERS
        place = lax.broadcasted_iota(jnp.int32, (8, 1), 0)
        trace = small_m[0, 1:2, :]
        for j in range(1, NM):
            trace = trace + small_m[j, 1:2, :]
        norm = (MEMBERS + jnp.sum(trace, axis=1, keepdims=True)) / MEMBERS
        norms[...] = jnp.broadcast_to(norm, (8, 128))

        def own_rows(block):
            return [
                jnp.sum(jnp.where(place == 2 * y + i, block, 0.0), axis=0, keepdims=True)
                for i in range(2)
            ]

        centers[:2, :] = jnp.concatenate(own_rows(jnp.broadcast_to(center, (8, 128))), axis=0)
        for j in range(NM):
            vec[j] = jnp.concatenate(
                own_rows(ensemble_in[j] - center)
                + [small_m[j, 0:1, :], jnp.zeros((VR - 3, CM), jnp.float32)],
                axis=0,
            )

    def share_prev(i):
        arrive(prev_copies[i])
        rows = prev.at[prev_rows[i]]
        if i == 0:
            shared_copies.append(start([(rows, rows, sibling)], prev.at[pl.ds(0, CM)]))
        else:
            start([(rows, rows, sibling)], None, shared_copies[0])

    def whiten_prev():
        arrive(shared_copies[0])

        @pl.loop(0, HALF // KT)
        def _(s):
            here = pl.ds(pl.multiple_of(s * KT, KT), KT)
            at = pl.ds(pl.multiple_of(half + s * KT, KT), KT)
            white_prev[:, here] = whiten(prev[:, here], at)

    usual = (reduce_y, reduce_z, spread_z, spread_y, finish)
    short = (reduce_y, exchange_z, spread_sum, finish)
    state = [None] * n
    small_state = None
    for item in ORDER:
        if item == "prev 0":
            share_prev(0)
        elif item == "prev 1":
            share_prev(1)
        elif item == "white prev":
            whiten_prev()
        elif item == "small":
            small_state = small_sums(None)
        elif item == "small y":
            small_state = small_sum_y(small_state)
        elif item == "small z":
            small_state = small_sum_z(small_state)
        elif item == "vectors":
            first_vectors(small_state)
        else:
            q, stage = item
            state[q] = (short if ROWS[q] == SHORT else usual)[stage](q, state[q])

    norm = norms[:1, :1]

    def folded(rows):
        return rows[:VR] + rows[VR : 2 * VR] + rows[2 * VR : 3 * VR]

    behind = ((c + NX - 1) % NX) * 2
    ring = [x_pair(2, core) for core in range(2)]

    def times(step):
        ahead = vec[((c + 1) % NX) * 2 + k]
        down = stacked(jnp.concatenate([vec[mem], ahead], axis=1), 4 * VR)
        across = stacked(jnp.concatenate([vec[2 * c], vec[2 * c + 1]], axis=1), 4 * VR)
        back = stacked(jnp.concatenate([vec[behind], vec[behind + 1]], axis=1), 4 * VR)
        for_next = for_own = for_last = 0.0
        for i in range(3):
            for_next = for_next + times_gram(across, terms[i, CM : 2 * CM, :])
            for_next = for_next + times_gram(back, terms[i, 2 * CM :, :])
            for_last = for_last + jnp.dot(
                down[:, CM:], terms[i, 2 * CM :, :], preferred_element_type=jnp.float32
            )
        exchange[step, mem, :, :CM] = folded(for_next)
        exchange[step, mem, :, 3 * CM :] = folded(for_last)

        def same(first, count, device):
            here = exchange.at[step, mem, :, pl.ds(pl.multiple_of(first * CM, CM), count * CM)]
            return here, here, device

        def pair(first, count, chips):
            return [same(first, count, x_pair(chips, core)) for core in range(2)]

        needed = start(
            pair(0, 1, 2) + [same(3 + core, 1, device) for core, device in enumerate(ring)],
            tally.at[pl.ds(0, 22)],
        )
        for i in range(3):
            for_own = for_own + jnp.dot(
                down, terms[i, : 2 * CM, :], preferred_element_type=jnp.float32
            )
        exchange[step, mem, :, CM : 3 * CM] = folded(for_own)
        mine = pl.ds(pl.multiple_of((k + 1) * CM, CM), CM)
        exchange[step, mem, :, mine] += vec[mem]
        start(pair(0, 3, 1) + pair(1, 4, -1) + [same(1, 4, sibling)], None, needed)
        if step == 1:
            return needed, None
        late = start(
            pair(1, 2, 2)
            + [same(4 - core, 1, device) for core, device in enumerate(ring)]
            + pair(3, 2, 1)
            + pair(0, 1, -1)
            + [same(0, 1, sibling)],
            tally.at[pl.ds(0, 13)],
        )
        return needed, late

    def product(step, chip, core):
        mine = pl.ds(pl.multiple_of((core + 1) * CM, CM), CM)
        last = pl.ds(pl.multiple_of((core + 3) * CM, CM), CM)
        below, above = 2 * ((chip + NX - 1) % NX), 2 * ((chip + 1) % NX)
        at = 2 * chip
        whole = (
            exchange[step, below + core, :, pl.ds(0, CM)]
            + exchange[step, at, :, mine]
            + exchange[step, at + 1, :, mine]
            + exchange[step, above, :, last]
            + exchange[step, above + 1, :, last]
        )
        return whole / norm

    neighbours = [(c, 0), (c, 1), ((c + 1) % NX, k), ((c + NX - 1) % NX, 0), ((c + NX - 1) % NX, 1)]
    distant = [((c + 1) % NX, 1 - k), ((c + 2) % NX, 0), ((c + 2) % NX, 1)]

    def advanced(step, pieces, update):
        for chip, core in pieces:
            at = 2 * chip + core
            vec[at] = update(vec[at], product(step, chip, core))

    def one_step(old, value):
        return 1.5 * old - 0.5 * value

    needed, late = times(0)
    arrive(needed)
    advanced(0, neighbours, one_step)
    for chip, core in neighbours:
        polys[2 * chip + core] = vec[2 * chip + core]
    before = len(started)
    needed, _ = times(1)
    drain(before)
    arrive(late)
    advanced(0, distant, one_step)
    for chip, core in distant:
        polys[2 * chip + core] = vec[2 * chip + core]
    arrive(needed)
    advanced(1, neighbours, one_step)
    needed, late = times(2)
    arrive(needed)
    advanced(2, neighbours, lambda old, value: value)
    needed, last = times(3)
    arrive(late)
    advanced(2, distant, lambda old, value: value)
    arrive(needed)
    arrive(last)
    shift = jnp.zeros((2, 1), jnp.float32)
    for chip in range(NX):
        for core in range(2):
            at = 2 * chip + core
            applied = 1.5 * polys[at] - 0.5 * (1.5 * vec[at] - 0.5 * product(3, chip, core))
            polys[at] = applied
            shift = shift + jnp.sum(applied[:2] * applied[2:3], axis=1, keepdims=True)
    shift = shift / norm / math.sqrt(MEMBERS - 1)
    rows_out[y, :2, :] = centers[:2, :1] + shift + polys[mem][:2] / jnp.sqrt(norm)
    here = rows_out.at[y]
    arrive(start([(here, here, y_at(j)) for j in range(1, NY)], rows_out.at[pl.ds(0, NY - 1)]))
    plane[...] = jnp.concatenate([rows_out[j, :2, :] for j in range(NY)], axis=0)
    here = out_ref.at[group]
    planes = start([(plane, here, z_at(j)) for j in FAR_Z], out_ref.at[pl.ds(0, 8 * (NZ - 1))])
    stored = pltpu.make_async_copy(plane, here, loads.at[0])
    stored.start()
    arrive(planes)
    stored.wait()
    drain(len(started))


def shards(modelled_reactions, observations, noise_class, class_variance, ensemble):
    f32, bf16 = jnp.float32, jnp.bfloat16
    hbm = pl.BlockSpec(memory_space=pltpu.HBM)
    scratch = [
        pltpu.VMEM((NS, CM), bf16),
        pltpu.VMEM((1, NS), f32),
        pltpu.VMEM((1, NS), jnp.int32),
        pltpu.SMEM((8,), f32),
        pltpu.VMEM((CM, NS), bf16),
        pltpu.VMEM((CM, NS), bf16),
        pltpu.VMEM((2 * CM, HALF), bf16),
        pltpu.VMEM((CM, NS), bf16),
        pltpu.VMEM((2 * CM, NS), bf16),
        pltpu.VMEM((2 * CM, HALF), bf16),
        pltpu.VMEM((NM, 1, NS), f32),
        pltpu.VMEM((1, NS), f32),
        pltpu.VMEM((1, NS), f32),
        pltpu.VMEM((NM, 8, CM), f32),
        pltpu.VMEM((8, 128), f32),
        pltpu.VMEM((8, CM), f32),
        pltpu.VMEM((NY - 1, 8, CM), f32),
        pltpu.VMEM((NZ, 8, CM), f32),
        pltpu.VMEM((NM, 8, CM), f32),
        pltpu.VMEM((3 * CM, 512), f32),
        pltpu.VMEM((3, 3 * CM, 512), bf16),
        pltpu.VMEM((NM, VR, CM), f32),
        pltpu.VMEM((NM, VR, CM), f32),
        pltpu.VMEM((4, NM, VR, WIDE), f32),
        pltpu.VMEM((NY, 8, CM), f32),
        pltpu.VMEM((8, CM), f32),
        pltpu.VMEM((8, 128), f32),
        pltpu.VMEM((22, VR, CM), f32),
        pltpu.SemaphoreType.DMA((N_LOADS,)),
        pltpu.SemaphoreType.DMA((OWN + POOL,)),
        pltpu.SemaphoreType.DMA((N_SEMS,)),
    ]
    scratch += [pltpu.VMEM((r, 512), f32) for r in ROWS]
    scratch += [pltpu.VMEM((NY - 1, r // 4, 512), f32) for r in ROWS]
    scratch += [pltpu.VMEM((r // 4, 512), f32) for r in ROWS]
    scratch += [pltpu.VMEM((NZ - 1,) + piece_shape(r), f32) for r in ROWS]
    scratch += [pltpu.VMEM((r // 4, 512), f32) for r in ROWS]
    return pl.pallas_call(
        kernel,
        out_shape=jax.ShapeDtypeStruct((64, CM), f32),
        in_specs=[hbm] * 5,
        out_specs=hbm,
        scratch_shapes=scratch,
        compiler_params=pltpu.CompilerParams(
            collective_id=0, has_side_effects=True, vmem_limit_bytes=60 * 1024 * 1024
        ),
    )(
        class_variance,
        modelled_reactions,
        observations.reshape(1, NS),
        noise_class.reshape(1, NS),
        ensemble,
    )


def solution(mesh):
    placed = (P("dp", "mem"), P("dp"), P("dp"), P(), P(None, "mem"))
    return jax.shard_map(
        shards, mesh=mesh, in_specs=placed, out_specs=P(None, "mem"), check_vma=False
    )
```
